768 devices in a mesh: dst: 64 (over x, y, core), src: 12 (over z).
Axes of the slice: x: 4, y: 8, z: 12, core: 2. Of those that a mesh axis runs over, the one named last changes fastest.
Arguments:
- node_hidden_state: bfloat16 [24576, 256], P(('dst', 'src')), may hold values from -6 to 6
- self_projection_weight: bfloat16 [256, 256], replicated, may hold values from -0.375 to 0.375
- weight_value: bfloat16 [256, 256], replicated, may hold values from -0.375 to 0.375
- weight_edge: bfloat16 [256, 8], replicated, may hold values from -0.375 to 0.375
- weight_target: bfloat16 [256, 8], replicated, may hold values from -0.375 to 0.375
- layer_norm_gain: float32 [256], replicated, may hold values from 0.25 to 1.75
- edge_scale: float32 [8], replicated, may hold values from 0.5 to 2
- tile_index: int32 [64, 12, 8, 2], P('dst', 'src'), may hold values from 0 to 15, as said below
- tile_count: int32 [64, 12], P('dst', 'src'), may hold values from 2 to 8, as said below
- edge_feature: bfloat16 [64, 12, 8, 8, 128, 128], P('dst', 'src'), may hold values from -6 to 6
- edge_mask: int32 [64, 12, 8, 128, 128], P('dst', 'src'), may hold values from 0 to 1, as said below
- cotangent: bfloat16 [24576, 256], P(('dst', 'src')), may hold values from -6 to 6
Outputs:
- updated_node_features: bfloat16 [24576, 256], P(('dst', 'src'))
- node_grad: float32 [24576, 256], P(('dst', 'src'))
- edge_grad: bfloat16 [64, 12, 8, 8, 128, 128], P('dst', 'src')
The draws below stay inside these ranges and needn't reach their ends.
Inputs may be any that keep to these rules, and one draw needn't show every extreme that they name: `tile_index`: within one device's slots the pairs are distinct; the first entry is a row block below 3, the second a column block below 16; slots at or after the device's tile_count are padding. `tile_count`: number of live slots of each device; some device has all 8 live. `edge_mask`: some destination nodes have no edges in any tile.
All inputs are finite; a program needn't handle non-finite values.
Results may differ from the reference program's by a relative error of at most 0.0065.
Values may be sent and summed in bfloat16 or wider, within the bound.
A program may use at most 32 MiB of HBM per device.

```python
import math
import jax
import jax.numpy as jnp
from jax import lax

D = 256
HEADS = 8
TB = 128
RB_DEV = 3
TILES = 8
NODES = 24576
NODE_DEV = 32
GROUP = 2048
CB_GRP = 16
N_DST = 64
N_SRC = 12


def owner_row():
    holder = (CB_GRP - 1) * TB // NODE_DEV
    return (holder + N_DST // 2) % N_DST


def draw_tile_index(key, part):
    key = jax.random.fold_in(key, 11)
    keys = jax.random.split(key, N_DST * N_SRC)
    idents = jnp.arange(N_DST * N_SRC, dtype=jnp.int32)
    owner = owner_row()
    first_slot = jnp.arange(TILES, dtype=jnp.int32) == 0

    def pick_pairs(single, ident):
        first, second = jax.random.split(single)
        picks = jax.random.permutation(first, RB_DEV * (CB_GRP - 1))[:TILES].astype(jnp.int32)
        rows = picks // (CB_GRP - 1)
        cols = picks % (CB_GRP - 1)
        private_row = jax.random.randint(second, (), 0, RB_DEV, dtype=jnp.int32)
        chosen = jnp.logical_and(ident // N_SRC == owner, first_slot)
        rows = jnp.where(chosen, private_row, rows)
        cols = jnp.where(chosen, CB_GRP - 1, cols)
        return jnp.stack([rows, cols], axis=-1).astype(jnp.int32)
    pairs = jax.vmap(pick_pairs)(keys, idents)
    return pairs.reshape(N_DST, N_SRC, TILES, 2).astype(jnp.int32)


def draw_tile_count(key, part):
    key = jax.random.fold_in(key, 23)
    first, second = jax.random.split(key)
    lowest = max(1, TILES // 4)
    counts = jax.random.randint(first, (N_DST * N_SRC,), lowest, TILES + 1, dtype=jnp.int32)
    fullest = jax.random.randint(second, (), 0, N_DST * N_SRC, dtype=jnp.int32)
    counts = jnp.where(jnp.arange(N_DST * N_SRC, dtype=jnp.int32) == fullest, TILES, counts)
    return counts.reshape(N_DST, N_SRC).astype(jnp.int32)


def draw_edge_mask(key, part):
    key = jax.random.fold_in(key, 37)
    first, second = jax.random.split(key)
    keys = jax.random.split(first, N_DST)

    def shuffle_rows(single):
        return jax.random.permutation(single, TB).astype(jnp.int32)
    shuffled = jax.vmap(shuffle_rows)(keys)
    ranks = jnp.argsort(shuffled, axis=-1).astype(jnp.int32)
    dead_rows = max(1, TB // 32)
    sparse_rows = max(1, TB // 16)
    limits = jnp.where(ranks < dead_rows, 0, jnp.where(ranks < dead_rows + sparse_rows, 1, 8)).astype(jnp.int32)
    limits = jnp.broadcast_to(limits[:, None, None, :, None], (N_DST, 1, TILES, TB, 1))
    owner = owner_row()
    chosen = jnp.logical_and(jnp.arange(N_DST, dtype=jnp.int32)[:, None, None, None, None] == owner, jnp.arange(TILES, dtype=jnp.int32)[None, None, :, None, None] == 0)
    limits = jnp.where(chosen, 256, limits).astype(jnp.int32)
    drawn = jax.random.randint(second, (N_DST, N_SRC, TILES, TB, TB), 0, 2048, dtype=jnp.int32)
    return (drawn < limits).astype(jnp.int32)


def shard_levels(stream_key, extent, cuts, least, top_value):
    gain = 1.0
    for dim, shards_of in cuts:
        steps = jax.random.uniform(jax.random.fold_in(jax.random.fold_in(stream_key, 6), dim), (shards_of,), jnp.float32, least / len(cuts), top_value / len(cuts))
        gain = gain * jnp.repeat(jnp.exp(steps), extent[dim] // shards_of).reshape((-1,) + (1,) * (len(extent) - 1 - dim))
    return gain


def gaussian(own_key, extent, scale, limit, cuts=(), held_as=jnp.bfloat16):
    result = jax.random.normal(own_key, extent, jnp.float32) * scale
    if len(cuts) > 0:
        result = shard_levels(own_key, extent, cuts, -0.22, 0.18) * result
    return jnp.clip(result, min=-limit, max=limit).astype(held_as)


def setup_inputs(seed: int = 0) -> dict:
    seeds = jax.random.split(jax.random.key(seed), 13)
    node_hidden_state = gaussian(seeds[0], (NODES, D), 1.0, 6.0, ((0, 768),))
    self_projection_weight = gaussian(seeds[1], (D, D), D ** -0.5, 0.375)
    weight_value = gaussian(seeds[2], (D, D), D ** -0.5, 0.375)
    weight_edge = gaussian(seeds[3], (D, HEADS), D ** -0.5, 0.375)
    weight_target = gaussian(seeds[4], (D, HEADS), D ** -0.5, 0.375)
    layer_norm_gain = jnp.clip(1.0 + 0.15 * jax.random.normal(seeds[5], (D,), jnp.float32), 0.25, 1.75)
    edge_scale = jnp.clip(jnp.exp(jax.random.uniform(seeds[6], (HEADS,), jnp.float32, math.log(0.5), math.log(2.0))), 0.5, 2.0)
    tile_index = draw_tile_index(jax.random.fold_in(seeds[12], 71), 0)
    tile_count = draw_tile_count(jax.random.fold_in(seeds[12], 71), 0)
    edge_feature = gaussian(seeds[9], (N_DST, N_SRC, TILES, HEADS, TB, TB), 1.0, 6.0, ((0, 64), (1, 12)))
    edge_mask = draw_edge_mask(jax.random.fold_in(seeds[12], 71), 0)
    cotangent = gaussian(seeds[11], (NODES, D), 1.0, 6.0, ((0, 768),))
    return dict(node_hidden_state=node_hidden_state, self_projection_weight=self_projection_weight, weight_value=weight_value, weight_edge=weight_edge, weight_target=weight_target, layer_norm_gain=layer_norm_gain, edge_scale=edge_scale, tile_index=tile_index, tile_count=tile_count, edge_feature=edge_feature, edge_mask=edge_mask, cotangent=cotangent)


def node_update_forward(state, numerator_total, denominator_total, self_projection_weight, layer_norm_gain):
    count = state.shape[0]
    denominator_floor = denominator_total + 1.0
    agg = (numerator_total.reshape(count, HEADS, -1) / denominator_floor[:, :, None]).reshape(count, -1)
    pre = jnp.dot(state, self_projection_weight, preferred_element_type=jnp.float32) + agg
    centred_values = pre - lax.optimization_barrier(jnp.mean(pre, axis=-1, keepdims=True))
    inverse_scale = lax.rsqrt(lax.optimization_barrier(jnp.mean(centred_values * centred_values, axis=-1, keepdims=True)) + 1e-05)
    normalized_input = centred_values * inverse_scale
    normed_output = normalized_input * layer_norm_gain
    updated_node_features = (state.astype(jnp.float32) + jax.nn.silu(normed_output)).astype(jnp.bfloat16)
    return (updated_node_features, denominator_floor, normalized_input, inverse_scale, normed_output)

def node_update_backward(cotangent, normed_output, normalized_input, inverse_scale, layer_norm_gain, numerator_total, denominator_total, denominator_floor):
    count = cotangent.shape[0]
    logistic = jax.nn.sigmoid(normed_output)
    grad_y = cotangent.astype(jnp.float32) * logistic * (1.0 + normed_output * (1.0 - logistic))
    normed_input_gradient = grad_y * layer_norm_gain
    preactivation_gradient = inverse_scale * (normed_input_gradient - lax.optimization_barrier(jnp.mean(normed_input_gradient, axis=-1, keepdims=True)) - normalized_input * lax.optimization_barrier(jnp.mean(normed_input_gradient * normalized_input, axis=-1, keepdims=True)))
    numerator_gradient = (preactivation_gradient.reshape(count, HEADS, -1) / denominator_floor[:, :, None]).reshape(count, -1).astype(jnp.bfloat16)
    inner = lax.optimization_barrier(jnp.sum((preactivation_gradient * numerator_total).reshape(count, HEADS, -1), axis=-1))
    denominator_gradient = (-inner / (denominator_floor * denominator_floor)).astype(jnp.bfloat16)
    return (preactivation_gradient, numerator_gradient, denominator_gradient)

def reference(node_hidden_state, self_projection_weight, weight_value, weight_edge, weight_target, layer_norm_gain, edge_scale, tile_index, tile_count, edge_feature, edge_mask, cotangent):
    f32 = jnp.float32
    low = jnp.bfloat16
    size_head = D // HEADS
    zero = jnp.zeros((), jnp.int32)
    value = jnp.dot(node_hidden_state, weight_value, preferred_element_type=f32).astype(low)
    source_gate = jnp.dot(node_hidden_state, weight_edge, preferred_element_type=f32).astype(low)
    target_gate = jnp.dot(node_hidden_state, weight_target, preferred_element_type=f32).astype(low)

    def grouped(array):
        width = array.shape[-1]
        return array.reshape(N_DST, N_SRC, NODE_DEV, width).transpose(1, 0, 2, 3).reshape(N_SRC, GROUP, width)

    def ungrouped(array):
        width = array.shape[-1]
        return array.reshape(N_SRC, N_DST, NODE_DEV, width).transpose(1, 0, 2, 3).reshape(NODES, width)
    value_group = grouped(value)
    gate_group = grouped(source_gate)
    total_slots = N_DST * N_SRC * TILES
    order = jnp.arange(total_slots, dtype=jnp.int32)
    device = order // TILES
    slot = order % TILES
    dst_of = (device // N_SRC).astype(jnp.int32)
    src_of = (device % N_SRC).astype(jnp.int32)
    alive = (slot < tile_count.reshape(-1)[device]).astype(f32)
    flat_index = tile_index.reshape(total_slots, 2).astype(jnp.int32)
    flat_feat = edge_feature.reshape(total_slots, HEADS, TB, TB)
    flat_mask = edge_mask.reshape(total_slots, TB, TB)
    items = (dst_of, src_of, flat_index, flat_feat, flat_mask, alive)

    def tile_common(item):
        dst_id, src_id, pair, feat, mask_tile, flag = item
        row0 = (dst_id * (RB_DEV * TB) + pair[0] * TB).astype(jnp.int32)
        col0 = (pair[1] * TB).astype(jnp.int32)
        vals = lax.dynamic_slice(value_group, (src_id, col0, zero), (1, TB, D))[0].reshape(TB, HEADS, size_head)
        src_rows = lax.dynamic_slice(gate_group, (src_id, col0, zero), (1, TB, HEADS))[0]
        dst_rows = lax.dynamic_slice(target_gate, (row0, zero), (TB, HEADS))
        sigma = jax.nn.sigmoid(edge_scale[:, None, None] * feat.astype(f32) + src_rows.astype(f32).T[:, None, :] + dst_rows.astype(f32).T[:, :, None])
        weight = mask_tile.astype(f32) * flag
        gate = sigma * weight[None]
        return (row0, col0, src_id, vals, sigma, weight, gate)

    def forward_step(carry, item):
        numerator_total, denominator_total = carry
        row0, col0, src_id, vals, sigma, weight, gate = tile_common(item)
        gate_low = gate.astype(low)
        tile_num = jnp.einsum('kij,jke->ike', gate_low.astype(f32), vals.astype(f32)).reshape(TB, D)
        tile_den = lax.optimization_barrier(jnp.sum(gate, axis=2)).T
        numerator_total = lax.dynamic_update_slice(numerator_total, lax.dynamic_slice(numerator_total, (row0, zero), (TB, D)) + tile_num, (row0, zero))
        denominator_total = lax.dynamic_update_slice(denominator_total, lax.dynamic_slice(denominator_total, (row0, zero), (TB, HEADS)) + tile_den, (row0, zero))
        return ((numerator_total, denominator_total), None)
    start = (jnp.zeros((NODES, D), f32), jnp.zeros((NODES, HEADS), f32))
    (numerator_total, denominator_total), unused = lax.scan(forward_step, start, items)
    updated_node_features, denominator_floor, normalized_input, inverse_scale, normed_output = node_update_forward(node_hidden_state, numerator_total, denominator_total, self_projection_weight, layer_norm_gain)
    preactivation_gradient, numerator_gradient, denominator_gradient = node_update_backward(cotangent, normed_output, normalized_input, inverse_scale, layer_norm_gain, numerator_total, denominator_total, denominator_floor)

    def backward_step(carry, item):
        grad_value, grad_gate, grad_target = carry
        row0, col0, src_id, vals, sigma, weight, gate = tile_common(item)
        gate_low = gate.astype(low)
        num_rows = lax.dynamic_slice(numerator_gradient, (row0, zero), (TB, D)).astype(f32).reshape(TB, HEADS, size_head)
        den_rows = lax.dynamic_slice(denominator_gradient, (row0, zero), (TB, HEADS)).astype(f32)
        grad_sig = jnp.einsum('ike,jke->kij', num_rows, vals.astype(f32)) + den_rows.T[:, :, None]
        tile_value = jnp.einsum('kij,ike->jke', gate_low.astype(f32), num_rows).reshape(TB, D)
        grad_logit = grad_sig * weight[None] * sigma * (1.0 - sigma)
        grad_tile = (grad_logit * edge_scale[:, None, None]).astype(low)
        tile_gate = lax.optimization_barrier(jnp.sum(grad_logit, axis=1)).T
        tile_target = lax.optimization_barrier(jnp.sum(grad_logit, axis=2)).T
        old_value = lax.dynamic_slice(grad_value, (src_id, col0, zero), (1, TB, D))
        grad_value = lax.dynamic_update_slice(grad_value, old_value + tile_value[None], (src_id, col0, zero))
        old_gate = lax.dynamic_slice(grad_gate, (src_id, col0, zero), (1, TB, HEADS))
        grad_gate = lax.dynamic_update_slice(grad_gate, old_gate + tile_gate[None], (src_id, col0, zero))
        old_target = lax.dynamic_slice(grad_target, (row0, zero), (TB, HEADS))
        grad_target = lax.dynamic_update_slice(grad_target, old_target + tile_target, (row0, zero))
        return ((grad_value, grad_gate, grad_target), grad_tile)
    start = (jnp.zeros((N_SRC, GROUP, D), f32), jnp.zeros((N_SRC, GROUP, HEADS), f32), jnp.zeros((NODES, HEADS), f32))
    (grad_value, grad_gate, grad_target), grad_tiles = lax.scan(backward_step, start, items)
    grad_value = ungrouped(grad_value)
    grad_gate = ungrouped(grad_gate)
    node_grad = cotangent.astype(f32) + jnp.dot(preactivation_gradient.astype(low), self_projection_weight.T, preferred_element_type=f32) + jnp.dot(grad_value.astype(low), weight_value.T, preferred_element_type=f32) + jnp.dot(grad_gate.astype(low), weight_edge.T, preferred_element_type=f32) + jnp.dot(grad_target.astype(low), weight_target.T, preferred_element_type=f32)
    edge_grad = grad_tiles.reshape(N_DST, N_SRC, TILES, HEADS, TB, TB)
    return (updated_node_features, node_grad, edge_grad)
```

```python
import functools

import jax
import jax.numpy as jnp
from jax import lax
from jax.experimental import pallas as pl
from jax.experimental.pallas import tpu as pltpu
from jax.sharding import PartitionSpec as P

F32 = jnp.float32
LOW = jnp.bfloat16
D = 256
HEADS = 8
HALF = 4
TB = 128
SH = D // HEADS
MESH = pl.DeviceIdType.MESH
NT = (((1,), (1,)), ((), ()))


def mm(a, b):
    return jnp.dot(a, b, preferred_element_type=F32)


def mm_nt(a, b):
    return lax.dot_general(a, b, NT, preferred_element_type=F32)


def mm_exact(a, b):
    return jnp.dot(a, b, preferred_element_type=F32, precision=lax.Precision.HIGHEST)


def iota(shape, dim):
    return lax.broadcasted_iota(jnp.int32, shape, dim)


def kernel(
    shape,
    scale_ref, pair_ref, count_ref,
    h_ref, cot_ref, wet_ref, wtt_ref, gain_ref,
    wself_hbm, wvalue_hbm, feat_hbm, mask_hbm,
    out_ref, grad_ref, edge_hbm,
    wself, wvalue, feat, mask, hbuf, tbuf, gate32, gate16, vmask, nt, onehot, spread,
    send0, send1, recv0, recv1, dbuf, dnt, egbuf, pt, wproj, lut, dtbuf,
    dpart, rcore, s1, rx, s2, ry, dtsend, dtrecv,
    lsem, esem,
    ysend, yrecv, xsend, xrecv, csend, crecv, tsend, trecv,
    z0send, z0recv, z1send, z1recv, dsend, drecv,
    bcsend, bcrecv, bxsend, bxrecv, bysend, byrecv, gsend, grecv,
):
    nx, ny, nz, nd, slots = shape
    rb = nz * nd // TB
    cb = nx * ny * 2 * nd // TB
    cbx = cb // nx
    dst = lax.axis_index("dst")
    z = lax.axis_index("src")
    x = dst // (ny * 2)
    y = lax.rem(dst // 2, ny)
    c = lax.rem(dst, 2)

    def at_y(v):
        return {"dst": (x * ny + v) * 2 + c, "src": z}

    def at_x(v):
        return {"dst": (v * ny + y) * 2 + c, "src": z}

    def at_z(v):
        return {"dst": dst, "src": v}

    sibling = {"dst": (x * ny + y) * 2 + 1 - c, "src": z}

    def remote(src, dst_ref, ssem, rsem, device):
        return pltpu.make_async_remote_copy(
            src_ref=src, dst_ref=dst_ref, send_sem=ssem, recv_sem=rsem,
            device_id=device, device_id_type=MESH,
        )

    loads = [
        pltpu.make_async_copy(wvalue_hbm, wvalue, lsem.at[0]),
        pltpu.make_async_copy(wself_hbm, wself, lsem.at[1]),
        pltpu.make_async_copy(mask_hbm.at[0, 0], mask, lsem.at[2]),
        pltpu.make_async_copy(feat_hbm.at[0, 0], feat, lsem.at[3]),
    ]
    for load in loads:
        load.start()

    barrier = pltpu.get_barrier_semaphore()
    for d in range(1, ny):
        pl.semaphore_signal(barrier, inc=1, device_id=at_y(lax.rem(y + d, ny)), device_id_type=MESH)
    for d in range(1, nx):
        pl.semaphore_signal(barrier, inc=1, device_id=at_x(lax.rem(x + d, nx)), device_id_type=MESH)
    for d in range(1, nz):
        pl.semaphore_signal(barrier, inc=1, device_id=at_z(lax.rem(z + d, nz)), device_id_type=MESH)
    pl.semaphore_signal(barrier, inc=1, device_id=sibling, device_id_type=MESH)

    h = h_ref[...]
    hbuf[x, y, c] = h
    wtt = jnp.concatenate([wtt_ref[...].astype(F32), jnp.zeros((TB - HEADS, D), F32)], axis=0).astype(LOW)
    wet32 = jnp.concatenate([wet_ref[...].astype(F32), jnp.zeros((TB - HEADS, D), F32)], axis=0)
    wet = wet32[:16].astype(LOW)
    tbuf[z] = mm_nt(h, wtt).astype(LOW)

    pl.semaphore_wait(barrier, ny + nx + nz - 2)

    for d in range(1, ny):
        remote(h_ref, hbuf.at[x, y, c], ysend.at[d], yrecv.at[d], at_y(lax.rem(y + d, ny))).start()
    for d in range(1, nz):
        remote(tbuf.at[z], tbuf.at[z], tsend.at[d], trecv.at[d], at_z(lax.rem(z + d, nz))).start()

    count = count_ref[0, 0]
    rows = [jnp.clip(pair_ref[0, 0, t, 0], 0, rb - 1) for t in range(slots)]
    cols = [jnp.clip(pair_ref[0, 0, t, 1], 0, cb - 1) for t in range(slots)]
    live = [jnp.where(count > t, 1.0, 0.0).astype(F32) for t in range(slots)]

    def fill_lut(q, carry):
        for r in range(rb):
            found = jnp.int32(slots)
            for t in range(slots):
                hit = (rows[t] == r) & (cols[t] == q) & (count > t)
                found = jnp.where(hit, jnp.int32(t), found)
            lut[q, r] = found
        return carry

    lax.fori_loop(0, cb, fill_lut, 0)
    lane = iota((TB, TB), 1)
    for half in range(2):
        for k in range(HALF):
            onehot[half, k * TB:(k + 1) * TB, :] = jnp.where(lane == half * HALF + k, 1.0, 0.0).astype(LOW)
            spread[half, :, k * TB:(k + 1) * TB] = jnp.where(
                iota((TB, TB), 0) == half * HALF + k, 0.5, 0.0
            ).astype(LOW)
    pt[slots] = jnp.zeros((TB, D), F32)
    loads[0].wait()
    wproj[:, 0:D] = wvalue[...]
    wproj[:, D:D + TB] = wet32.T.astype(LOW)
    loads[1].wait()
    self_pre = mm(h, wself[...])

    for d in range(1, ny):
        v = lax.rem(y + ny - d, ny)
        remote(hbuf.at[x, v, c], hbuf.at[x, v, c], ysend.at[d], yrecv.at[d], at_y(v)).wait_recv()
    for d in range(1, nx):
        remote(hbuf.at[x, :, c], hbuf.at[x, :, c], xsend.at[d], xrecv.at[d], at_x(lax.rem(x + d, nx))).start()
    remote(hbuf.at[x, :, c], hbuf.at[x, :, c], csend.at[0], crecv.at[0], sibling).start()
    for d in range(1, nx):
        v = lax.rem(x + nx - d, nx)
        remote(hbuf.at[v, :, c], hbuf.at[v, :, c], xsend.at[d], xrecv.at[d], at_x(v)).wait_recv()
        remote(hbuf.at[v, :, c], hbuf.at[v, :, c], csend.at[d], crecv.at[d], sibling).start()
    for d in range(1, nz):
        v = lax.rem(z + nz - d, nz)
        remote(tbuf.at[v], tbuf.at[v], tsend.at[d], trecv.at[d], at_z(v)).wait_recv()
    loads[2].wait()
    loads[3].wait()
    for d in range(nx):
        v = lax.rem(x + nx - d, nx)
        remote(hbuf.at[v, :, 1 - c], hbuf.at[v, :, 1 - c], csend.at[d], crecv.at[d], sibling).wait_recv()

    def h_tile(col):
        per = cbx
        xi = col // per
        q = lax.rem(col, per)
        step = ny // per
        return hbuf[xi, pl.ds(q * step, step)].reshape(TB, D)

    def tile_scalars(t):
        row = jnp.clip(pair_ref[0, 0, t, 0], 0, rb - 1)
        col = jnp.clip(pair_ref[0, 0, t, 1], 0, cb - 1)
        return row, col, jnp.where(count > t, 1.0, 0.0).astype(F32)

    lane_d = iota((TB, D), 1) // SH

    def t_rows(row):
        per = TB // nd
        return tbuf[pl.ds(row * per, per)].reshape(TB, TB)

    def forward(half):
        def step(t, carry):
            row, col, flag = tile_scalars(t)
            ht = h_tile(col)
            val = mm(ht, wvalue[:, half * TB:(half + 1) * TB])
            src = mm_nt(wet, ht).astype(LOW).astype(F32) * 0.5
            outer = mm(t_rows(row), spread[half])
            weight = mask[t].astype(F32) * flag
            gates = []
            for k in range(HALF):
                kk = half * HALF + k
                vmask[t, half, k * TB:(k + 1) * TB, :] = jnp.where(
                    lane // SH == k, val, 0.0
                ).astype(LOW)
                arg = feat[t, kk].astype(F32) * (scale_ref[kk] * 0.5) + (
                    outer[:, k * TB:(k + 1) * TB] + src[kk:kk + 1, :]
                )
                gate = (0.5 * jnp.tanh(arg) + 0.5) * weight
                gate32[t, kk] = gate
                low = gate.astype(LOW)
                gate16[t, kk] = low
                gates.append(low)
            rhs = jnp.concatenate([vmask[t, half], onehot[half]], axis=1)
            nt[half, t] = mm(jnp.concatenate(gates, axis=1), rhs)
            return carry

        lax.fori_loop(0, slots, step, 0)

    per = TB // nd

    def row_sums(lanes, parts):
        for r in range(rb):
            sel = [jnp.where(rows[t] == r, 1.0, 0.0).astype(F32) for t in range(slots)]
            total = jnp.zeros((TB, lanes), F32)
            for half, start in parts:
                for t in range(slots):
                    total += nt[half, t, :, start:start + lanes] * sel[t]
            yield r, total

    forward(0)
    for r, total in row_sums(TB, [(0, 0)]):
        send0[r * per:(r + 1) * per] = total.astype(LOW).reshape(per, nd, TB)
    for d in range(1, nz):
        v = lax.rem(z + d, nz)
        remote(send0.at[v], recv0.at[d], z0send.at[d], z0recv.at[d], at_z(v)).start()
    forward(1)
    for r, total in row_sums(TB, [(1, 0)]):
        send1[r * per:(r + 1) * per, :, 0:TB] = total.astype(LOW).reshape(per, nd, TB)
    for r, total in row_sums(TB, [(0, TB), (1, TB)]):
        send1[r * per:(r + 1) * per, :, TB:D] = total.astype(LOW).reshape(per, nd, TB)
    for d in range(1, nz):
        v = lax.rem(z + d, nz)
        remote(send1.at[v], recv1.at[d], z1send.at[d], z1recv.at[d], at_z(v)).start()

    def slope(t, carry):
        for k in range(HEADS):
            g = gate32[t, k]
            gate32[t, k] = g - g * g
        return carry

    lax.fori_loop(0, slots, slope, 0)

    num0 = send0[z].astype(F32)
    both = send1[z].astype(F32)
    for d in range(1, nz):
        remote(recv0.at[d], recv0.at[d], z0send.at[d], z0recv.at[d], at_z(z)).wait_recv()
        num0 += recv0[d].astype(F32)
    for d in range(1, nz):
        remote(recv1.at[d], recv1.at[d], z1send.at[d], z1recv.at[d], at_z(z)).wait_recv()
        both += recv1[d].astype(F32)

    num = jnp.concatenate([num0, both[:, 0:TB]], axis=1)
    floor = both[:, TB:D] + 1.0
    expand = jnp.where(iota((TB, D), 0) == lane_d, 1.0, 0.0).astype(F32)
    floor_d = mm_exact(floor, expand)
    pre = self_pre + num / floor_d
    centred = pre - jnp.mean(pre, axis=-1, keepdims=True)
    inv = lax.rsqrt(jnp.mean(centred * centred, axis=-1, keepdims=True) + 1e-05)
    xhat = centred * inv
    gain = gain_ref[...]
    yv = xhat * gain
    sg = jax.nn.sigmoid(yv)
    cot = cot_ref[...].astype(F32)
    out_ref[...] = (h.astype(F32) + yv * sg).astype(LOW)
    dx = cot * sg * (1.0 + yv * (1.0 - sg)) * gain
    dpre = inv * (
        dx - jnp.mean(dx, axis=-1, keepdims=True) - xhat * jnp.mean(dx * xhat, axis=-1, keepdims=True)
    )
    collect = jnp.where(iota((D, TB), 0) // SH == iota((D, TB), 1), 1.0, 0.0).astype(F32)
    dden = -mm_exact(dpre * num, collect) / (floor * floor)
    dbuf[z] = jnp.concatenate([dpre / floor_d, dden], axis=1).astype(LOW)
    for d in range(1, nz):
        remote(dbuf.at[z], dbuf.at[z], dsend.at[d], drecv.at[d], at_z(lax.rem(z + d, nz))).start()
    own_grad = cot + mm_nt(dpre.astype(LOW), wself[...])
    for d in range(1, nz):
        v = lax.rem(z + nz - d, nz)
        remote(dbuf.at[v], dbuf.at[v], dsend.at[d], drecv.at[d], at_z(v)).wait_recv()

    for r in range(rb):
        block = dbuf[r * per:(r + 1) * per, :, 0:D].reshape(TB, D).astype(F32)
        dnt[r] = block.T.astype(LOW)

    def backward(t, carry):
        row, col, flag = tile_scalars(t)
        dn = dbuf[pl.ds(row * per, per)].reshape(TB, D + TB)
        dnr = dnt[row]
        grads = []
        dt = jnp.zeros((TB, TB), F32)
        sums = []
        for half in range(2):
            lhs = jnp.concatenate([dn[:, half * TB:(half + 1) * TB], dn[:, D:D + TB]], axis=1)
            rhs = jnp.concatenate([vmask[t, half], onehot[half]], axis=1)
            dsig = mm_nt(lhs, rhs)
            lows = []
            for k in range(HALF):
                kk = half * HALF + k
                dl = dsig[:, k * TB:(k + 1) * TB] * gate32[t, kk]
                egbuf[t, kk] = (dl * scale_ref[kk]).astype(LOW)
                sums.append(jnp.sum(dl, axis=0, keepdims=True))
                lows.append(dl.astype(LOW))
                grads.append(mm(dnr[kk * SH:(kk + 1) * SH, :], gate16[t, kk]))
            dt += mm(jnp.concatenate(lows, axis=1), onehot[half])
        dtbuf[t] = dt
        pltpu.make_async_copy(egbuf.at[t], edge_hbm.at[0, 0, t], esem.at[t]).start()
        stack = jnp.concatenate(grads + sums + [jnp.zeros((TB - HEADS, TB), F32)], axis=0).astype(LOW)
        pt[t] = mm(wproj[...], stack).T
        return carry

    lax.fori_loop(0, slots, backward, 0)

    for r in range(rb):
        total = jnp.zeros((TB, TB), F32)
        for t in range(slots):
            total += dtbuf[t] * jnp.where(rows[t] == r, 1.0, 0.0).astype(F32)
        dtsend[r * per:(r + 1) * per] = total.astype(LOW).reshape(per, nd, TB)

    def quarter(xi):
        def one(q, carry):
            block = xi * cbx + q
            total = pt[lut[block, 0]]
            for r in range(1, rb):
                total += pt[lut[block, r]]
            step = ny // cbx
            dpart[xi, pl.ds(q * step, step)] = total.astype(LOW).reshape(step, 2, nd, D)
            return carry

        lax.fori_loop(0, cbx, one, 0)

    for d in range(nx):
        v = lax.rem(x + 1 + d, nx)
        quarter(v)
        remote(dpart.at[v, :, 1 - c], rcore.at[v], bcsend.at[d], bcrecv.at[d], sibling).start()
        if d == 0:
            for e in range(1, nz):
                w = lax.rem(z + e, nz)
                remote(dtsend.at[w], dtrecv.at[e], gsend.at[e], grecv.at[e], at_z(w)).start()
    for d in range(nx):
        v = lax.rem(x + 1 + d, nx)
        remote(rcore.at[v], rcore.at[v], bcsend.at[d], bcrecv.at[d], sibling).wait_recv()
        s1[v] = (dpart[v, :, c].astype(F32) + rcore[v].astype(F32)).astype(LOW)
        if d < nx - 1:
            remote(s1.at[v], rx.at[d], bxsend.at[d], bxrecv.at[d], at_x(v)).start()
    total = s1[x].astype(F32)
    for d in range(nx - 1):
        remote(rx.at[d], rx.at[d], bxsend.at[d], bxrecv.at[d], at_x(x)).wait_recv()
        total += rx[d].astype(F32)
    s2[...] = total.astype(LOW)
    for d in range(1, ny):
        v = lax.rem(y + d, ny)
        remote(s2.at[v], ry.at[d], bysend.at[d], byrecv.at[d], at_y(v)).start()
    dt = dtsend[z].astype(F32)
    for d in range(1, nz):
        remote(dtrecv.at[d], dtrecv.at[d], gsend.at[d], grecv.at[d], at_z(z)).wait_recv()
        dt += dtrecv[d].astype(F32)
    own_grad = own_grad + mm(dt.astype(LOW), wtt)
    final = s2[y].astype(F32)
    for d in range(1, ny):
        remote(ry.at[d], ry.at[d], bysend.at[d], byrecv.at[d], at_y(y)).wait_recv()
        final += ry[d].astype(F32)
    grad_ref[...] = own_grad + final

    for d in range(1, ny):
        remote(h_ref, h_ref, ysend.at[d], yrecv.at[d], at_y(y)).wait_send()
        remote(s2.at[y], s2.at[y], bysend.at[d], byrecv.at[d], at_y(y)).wait_send()
    for d in range(1, nx):
        remote(hbuf.at[x, :, c], hbuf.at[x, :, c], xsend.at[d], xrecv.at[d], at_x(x)).wait_send()
        remote(s1.at[x], s1.at[x], bxsend.at[d - 1], bxrecv.at[d - 1], at_x(x)).wait_send()
    for d in range(nx):
        remote(hbuf.at[x, :, c], hbuf.at[x, :, c], csend.at[d], crecv.at[d], sibling).wait_send()
        remote(rcore.at[x], rcore.at[x], bcsend.at[d], bcrecv.at[d], sibling).wait_send()
    for d in range(1, nz):
        remote(tbuf.at[z], tbuf.at[z], tsend.at[d], trecv.at[d], at_z(z)).wait_send()
        remote(send0.at[z], send0.at[z], z0send.at[d], z0recv.at[d], at_z(z)).wait_send()
        remote(send1.at[z], send1.at[z], z1send.at[d], z1recv.at[d], at_z(z)).wait_send()
        remote(dbuf.at[z], dbuf.at[z], dsend.at[d], drecv.at[d], at_z(z)).wait_send()
        remote(dtsend.at[z], dtsend.at[z], gsend.at[d], grecv.at[d], at_z(z)).wait_send()
    for t in range(slots):
        pltpu.make_async_copy(egbuf.at[t], edge_hbm.at[0, 0, t], esem.at[t]).wait()


def body(
    nx, ny,
    node_hidden_state, self_projection_weight, weight_value, weight_edge, weight_target,
    layer_norm_gain, edge_scale, tile_index, tile_count, edge_feature, edge_mask, cotangent,
):
    nd = node_hidden_state.shape[0]
    nz = lax.axis_size("src")
    slots = edge_mask.shape[2]
    rb = nz * nd // TB
    cb = nx * ny * 2 * nd // TB
    vmem = pl.BlockSpec(memory_space=pltpu.VMEM)
    smem = pl.BlockSpec(memory_space=pltpu.SMEM)
    hbm = pl.BlockSpec(memory_space=pl.ANY)
    scratch = [
        pltpu.VMEM((D, D), LOW),
        pltpu.VMEM((D, D), LOW),
        pltpu.VMEM((slots, HEADS, TB, TB), LOW),
        pltpu.VMEM((slots, TB, TB), jnp.int32),
        pltpu.VMEM((nx, ny, 2, nd, D), LOW),
        pltpu.VMEM((nz, nd, TB), LOW),
        pltpu.VMEM((slots, HEADS, TB, TB), F32),
        pltpu.VMEM((slots, HEADS, TB, TB), LOW),
        pltpu.VMEM((slots, 2, HALF * TB, TB), LOW),
        pltpu.VMEM((2, slots, TB, D), F32),
        pltpu.VMEM((2, HALF * TB, TB), LOW),
        pltpu.VMEM((2, TB, HALF * TB), LOW),
        pltpu.VMEM((nz, nd, TB), LOW),
        pltpu.VMEM((nz, nd, D), LOW),
        pltpu.VMEM((nz, nd, TB), LOW),
        pltpu.VMEM((nz, nd, D), LOW),
        pltpu.VMEM((nz, nd, D + TB), LOW),
        pltpu.VMEM((rb, D, TB), LOW),
        pltpu.VMEM((slots, HEADS, TB, TB), LOW),
        pltpu.VMEM((slots + 1, TB, D), F32),
        pltpu.VMEM((D, D + TB), LOW),
        pltpu.SMEM((cb, rb), jnp.int32),
        pltpu.VMEM((slots, TB, TB), F32),
        pltpu.VMEM((nx, ny, 2, nd, D), LOW),
        pltpu.VMEM((nx, ny, nd, D), LOW),
        pltpu.VMEM((nx, ny, nd, D), LOW),
        pltpu.VMEM((nx, ny, nd, D), LOW),
        pltpu.VMEM((ny, nd, D), LOW),
        pltpu.VMEM((ny, nd, D), LOW),
        pltpu.VMEM((nz, nd, TB), LOW),
        pltpu.VMEM((nz, nd, TB), LOW),
        pltpu.SemaphoreType.DMA((4,)),
        pltpu.SemaphoreType.DMA((slots,)),
    ]
    for n in (ny, nx, nx, nz, nz, nz, nz, nx, nx, ny, nz):
        scratch += [pltpu.SemaphoreType.DMA((n,)), pltpu.SemaphoreType.DMA((n,))]
    return pl.pallas_call(
        functools.partial(kernel, (nx, ny, nz, nd, slots)),
        out_shape=(
            jax.ShapeDtypeStruct((nd, D), LOW),
            jax.ShapeDtypeStruct((nd, D), F32),
            jax.ShapeDtypeStruct((1, 1, slots, HEADS, TB, TB), LOW),
        ),
        in_specs=[smem, smem, smem, vmem, vmem, vmem, vmem, vmem, hbm, hbm, hbm, hbm],
        out_specs=(vmem, vmem, hbm),
        scratch_shapes=scratch,
        compiler_params=pltpu.CompilerParams(
            collective_id=0, has_side_effects=True, vmem_limit_bytes=48 * 1024 * 1024
        ),
        name="gated_conv",
    )(
        edge_scale, tile_index, tile_count,
        node_hidden_state, cotangent, weight_edge.T, weight_target.T, layer_norm_gain[None, :],
        self_projection_weight, weight_value, edge_feature, edge_mask,
    )


def build(mesh, nx, ny):
    placed = (
        P(("dst", "src"), None), P(), P(), P(), P(), P(), P(),
        P("dst", "src", None, None), P("dst", "src"),
        P("dst", "src", None, None, None, None), P("dst", "src", None, None, None),
        P(("dst", "src"), None),
    )
    return jax.shard_map(
        functools.partial(body, nx, ny),
        mesh=mesh,
        in_specs=placed,
        out_specs=(
            P(("dst", "src"), None),
            P(("dst", "src"), None),
            P("dst", "src", None, None, None, None),
        ),
        check_vma=False,
    )


def solution(mesh):
    return build(mesh, 4, 8)
```

```python
import functools

import jax
import jax.numpy as jnp
from jax import lax
from jax.experimental import pallas as pl
from jax.experimental.pallas import tpu as pltpu
from jax.sharding import PartitionSpec as P

F32 = jnp.float32
LOW = jnp.bfloat16
D = 256
HEADS = 8
HALF = 4
TB = 128
SH = D // HEADS
MESH = pl.DeviceIdType.MESH
NT = (((1,), (1,)), ((), ()))


def mm(a, b):
    return jnp.dot(a, b, preferred_element_type=F32)


def mm_nt(a, b):
    return lax.dot_general(a, b, NT, preferred_element_type=F32)


def mm_exact(a, b):
    return jnp.dot(a, b, preferred_element_type=F32, precision=lax.Precision.HIGHEST)


def iota(shape, dim):
    return lax.broadcasted_iota(jnp.int32, shape, dim)


def kernel(
    shape,
    scale_hbm, pair_hbm, count_hbm,
    h_hbm, cot_hbm, wet_hbm, wtt_hbm, gain_hbm,
    wself_hbm, wvalue_hbm, feat_hbm, mask_hbm,
    out_ref, grad_ref, edge_hbm,
    scale_ref, pair_ref, count_ref, h_ref, cot_ref, wet_ref, wtt_ref, gain_ref,
    wself, wvalue, feat, mask, hbuf, tbuf, gate32, gate16, vmask, nt, onehot, spread,
    send0, send1, recv0, recv1, dbuf, dnt, egbuf, pt, wproj, lut, dtbuf,
    dpart, rcore, s1, rx, s2, ry, dtsend, dtrecv,
    lsem, esem,
    ysend, yrecv, xsend, xrecv, csend, crecv, tsend, trecv,
    z0send, z0recv, z1send, z1recv, dsend, drecv,
    bcsend, bcrecv, bxsend, bxrecv, bysend, byrecv, gsend, grecv,
):
    nx, ny, nz, nd, slots = shape
    rb = nz * nd // TB
    cb = nx * ny * 2 * nd // TB
    cbx = cb // nx
    dst = lax.axis_index("dst")
    z = lax.axis_index("src")
    x = dst // (ny * 2)
    y = lax.rem(dst // 2, ny)
    c = lax.rem(dst, 2)

    def at_y(v):
        return {"dst": (x * ny + v) * 2 + c, "src": z}

    def at_x(v):
        return {"dst": (v * ny + y) * 2 + c, "src": z}

    def at_z(v):
        return {"dst": dst, "src": v}

    sibling = {"dst": (x * ny + y) * 2 + 1 - c, "src": z}

    def remote(src, dst_ref, ssem, rsem, device):
        return pltpu.make_async_remote_copy(
            src_ref=src, dst_ref=dst_ref, send_sem=ssem, recv_sem=rsem,
            device_id=device, device_id_type=MESH,
        )

    small = [
        pltpu.make_async_copy(a, b, lsem.at[4 + i])
        for i, (a, b) in enumerate((
            (h_hbm, h_ref), (wtt_hbm, wtt_ref), (wet_hbm, wet_ref), (pair_hbm, pair_ref),
            (count_hbm, count_ref), (scale_hbm, scale_ref), (cot_hbm, cot_ref), (gain_hbm, gain_ref),
        ))
    ]
    for load in small:
        load.start()
    loads = [
        pltpu.make_async_copy(wvalue_hbm, wvalue, lsem.at[0]),
        pltpu.make_async_copy(wself_hbm, wself, lsem.at[1]),
        pltpu.make_async_copy(mask_hbm.at[0, 0], mask, lsem.at[2]),
        pltpu.make_async_copy(feat_hbm.at[0, 0], feat, lsem.at[3]),
    ]
    for load in loads:
        load.start()

    barrier = pltpu.get_barrier_semaphore()
    for d in range(1, ny):
        pl.semaphore_signal(barrier, inc=1, device_id=at_y(lax.rem(y + d, ny)), device_id_type=MESH)
    for d in range(1, nx):
        pl.semaphore_signal(barrier, inc=1, device_id=at_x(lax.rem(x + d, nx)), device_id_type=MESH)
    for d in range(1, nz):
        pl.semaphore_signal(barrier, inc=1, device_id=at_z(lax.rem(z + d, nz)), device_id_type=MESH)
    pl.semaphore_signal(barrier, inc=1, device_id=sibling, device_id_type=MESH)

    for load in small:
        load.wait()
    h = h_ref[...]
    hbuf[x, y, c] = h
    wtt = jnp.concatenate([wtt_ref[...].astype(F32), jnp.zeros((TB - HEADS, D), F32)], axis=0).astype(LOW)
    wet32 = jnp.concatenate([wet_ref[...].astype(F32), jnp.zeros((TB - HEADS, D), F32)], axis=0)
    wet = wet32[:16].astype(LOW)
    tbuf[z] = mm_nt(h, wtt).astype(LOW)

    pl.semaphore_wait(barrier, ny + nx + nz - 2)

    near = sorted(range(1, ny), key=lambda d: (min(d, ny - d), d))
    nearx = sorted(range(1, nx), key=lambda d: (min(d, nx - d), d))
    farz = sorted(range(1, nz), key=lambda d: (-min(d, nz - d), d))
    for d in near:
        remote(h_ref, hbuf.at[x, y, c], ysend.at[d], yrecv.at[d], at_y(lax.rem(y + d, ny))).start()
    for d in farz:
        remote(tbuf.at[z], tbuf.at[z], tsend.at[d], trecv.at[d], at_z(lax.rem(z + d, nz))).start()

    def block_out(d):
        v = lax.rem(y + ny - d, ny)
        block = hbuf.at[x, v, c]
        if d:
            remote(block, block, ysend.at[d], yrecv.at[d], at_y(v)).wait_recv()
        for e in reversed(nearx):
            remote(block, block, xsend.at[e, d], xrecv.at[e, d], at_x(lax.rem(x + e, nx))).start()
        remote(block, block, csend.at[0, d], crecv.at[0, d], sibling).start()

    block_out(0)

    count = count_ref[0, 0]
    rows = [jnp.clip(pair_ref[0, 0, 0, t], 0, rb - 1) for t in range(slots)]
    cols = [jnp.clip(pair_ref[0, 0, 1, t], 0, cb - 1) for t in range(slots)]
    live = [jnp.where(count > t, 1.0, 0.0).astype(F32) for t in range(slots)]

    def fill_lut(q, carry):
        for r in range(rb):
            found = jnp.int32(slots)
            for t in range(slots):
                hit = (rows[t] == r) & (cols[t] == q) & (count > t)
                found = jnp.where(hit, jnp.int32(t), found)
            lut[q, r] = found
        return carry

    lax.fori_loop(0, cb, fill_lut, 0)
    lane = iota((TB, TB), 1)
    for half in range(2):
        for k in range(HALF):
            onehot[half, k * TB:(k + 1) * TB, :] = jnp.where(lane == half * HALF + k, 1.0, 0.0).astype(LOW)
            spread[half, :, k * TB:(k + 1) * TB] = jnp.where(
                iota((TB, TB), 0) == half * HALF + k, 0.5, 0.0
            ).astype(LOW)
    pt[slots] = jnp.zeros((TB, D), F32)
    loads[0].wait()
    wproj[:, 0:D] = wvalue[...]
    wproj[:, D:D + TB] = wet32.T.astype(LOW)
    loads[1].wait()
    self_pre = mm(h, wself[...])

    for d in near:
        block_out(d)
    for d in [0] + near:
        v = lax.rem(y + ny - d, ny)
        for e in nearx:
            block = hbuf.at[lax.rem(x + nx - e, nx), v, c]
            remote(block, block, xsend.at[e, d], xrecv.at[e, d], sibling).wait_recv()
            remote(block, block, csend.at[e, d], crecv.at[e, d], sibling).start()
    for d in range(1, nz):
        v = lax.rem(z + nz - d, nz)
        remote(tbuf.at[v], tbuf.at[v], tsend.at[d], trecv.at[d], at_z(v)).wait_recv()
    loads[2].wait()
    loads[3].wait()
    for d in [0] + near:
        v = lax.rem(y + ny - d, ny)
        for e in [0] + nearx:
            block = hbuf.at[lax.rem(x + nx - e, nx), v, 1 - c]
            remote(block, block, csend.at[e, d], crecv.at[e, d], sibling).wait_recv()

    def h_tile(col):
        per = cbx
        xi = col // per
        q = lax.rem(col, per)
        step = ny // per
        return hbuf[xi, pl.ds(q * step, step)].reshape(TB, D)

    def tile_scalars(t):
        row = jnp.clip(pair_ref[0, 0, 0, t], 0, rb - 1)
        col = jnp.clip(pair_ref[0, 0, 1, t], 0, cb - 1)
        return row, col, jnp.where(count > t, 1.0, 0.0).astype(F32)

    lane_d = iota((TB, D), 1) // SH

    def t_rows(row):
        per = TB // nd
        return tbuf[pl.ds(row * per, per)].reshape(TB, TB)

    def forward(half):
        def step(t, carry):
            row, col, flag = tile_scalars(t)
            ht = h_tile(col)
            val = mm(ht, wvalue[:, half * TB:(half + 1) * TB])
            src = mm_nt(wet, ht).astype(LOW).astype(F32) * 0.5
            outer = mm(t_rows(row), spread[half])
            weight = mask[t].astype(F32) * flag
            gates = []
            for k in range(HALF):
                kk = half * HALF + k
                vmask[t, half, k * TB:(k + 1) * TB, :] = jnp.where(
                    lane // SH == k, val, 0.0
                ).astype(LOW)
                arg = feat[t, kk].astype(F32) * (scale_ref[kk] * 0.5) + (
                    outer[:, k * TB:(k + 1) * TB] + src[kk:kk + 1, :]
                )
                gate = (0.5 * jnp.tanh(arg) + 0.5) * weight
                gate32[t, kk] = gate
                low = gate.astype(LOW)
                gate16[t, kk] = low
                gates.append(low)
            rhs = jnp.concatenate([vmask[t, half], onehot[half]], axis=1)
            nt[half, t] = mm(jnp.concatenate(gates, axis=1), rhs)
            return carry

        lax.fori_loop(0, slots, step, 0)

    per = TB // nd

    def row_sums(lanes, parts):
        for r in range(rb):
            sel = [jnp.where(rows[t] == r, 1.0, 0.0).astype(F32) for t in range(slots)]
            total = jnp.zeros((TB, lanes), F32)
            for half, start in parts:
                for t in range(slots):
                    total += nt[half, t, :, start:start + lanes] * sel[t]
            yield r, total

    forward(0)
    for r, total in row_sums(TB, [(0, 0)]):
        send0[r * per:(r + 1) * per] = total.astype(LOW).reshape(per, nd, TB)
    for d in farz:
        v = lax.rem(z + d, nz)
        remote(send0.at[v], recv0.at[d], z0send.at[d], z0recv.at[d], at_z(v)).start()
    forward(1)
    for r, total in row_sums(TB, [(1, 0)]):
        send1[r * per:(r + 1) * per, :, 0:TB] = total.astype(LOW).reshape(per, nd, TB)
    for r, total in row_sums(TB, [(0, TB), (1, TB)]):
        send1[r * per:(r + 1) * per, :, TB:D] = total.astype(LOW).reshape(per, nd, TB)
    for d in farz:
        v = lax.rem(z + d, nz)
        remote(send1.at[v], recv1.at[d], z1send.at[d], z1recv.at[d], at_z(v)).start()

    def slope(t, carry):
        for k in range(HEADS):
            g = gate32[t, k]
            gate32[t, k] = g - g * g
        return carry

    lax.fori_loop(0, slots, slope, 0)

    num0 = send0[z].astype(F32)
    both = send1[z].astype(F32)
    for d in range(1, nz):
        remote(recv0.at[d], recv0.at[d], z0send.at[d], z0recv.at[d], at_z(z)).wait_recv()
        num0 += recv0[d].astype(F32)
    for d in range(1, nz):
        remote(recv1.at[d], recv1.at[d], z1send.at[d], z1recv.at[d], at_z(z)).wait_recv()
        both += recv1[d].astype(F32)

    num = jnp.concatenate([num0, both[:, 0:TB]], axis=1)
    floor = both[:, TB:D] + 1.0
    expand = jnp.where(iota((TB, D), 0) == lane_d, 1.0, 0.0).astype(F32)
    floor_d = mm_exact(floor, expand)
    pre = self_pre + num / floor_d
    centred = pre - jnp.mean(pre, axis=-1, keepdims=True)
    inv = lax.rsqrt(jnp.mean(centred * centred, axis=-1, keepdims=True) + 1e-05)
    xhat = centred * inv
    gain = gain_ref[...]
    yv = xhat * gain
    sg = jax.nn.sigmoid(yv)
    cot = cot_ref[...].astype(F32)
    out_ref[...] = (h.astype(F32) + yv * sg).astype(LOW)
    dx = cot * sg * (1.0 + yv * (1.0 - sg)) * gain
    dpre = inv * (
        dx - jnp.mean(dx, axis=-1, keepdims=True) - xhat * jnp.mean(dx * xhat, axis=-1, keepdims=True)
    )
    collect = jnp.where(iota((D, TB), 0) // SH == iota((D, TB), 1), 1.0, 0.0).astype(F32)
    dden = -mm_exact(dpre * num, collect) / (floor * floor)
    dbuf[z] = jnp.concatenate([dpre / floor_d, dden], axis=1).astype(LOW)
    for d in farz:
        remote(dbuf.at[z], dbuf.at[z], dsend.at[d], drecv.at[d], at_z(lax.rem(z + d, nz))).start()
    own_grad = cot + mm_nt(dpre.astype(LOW), wself[...])
    for d in range(1, nz):
        v = lax.rem(z + nz - d, nz)
        remote(dbuf.at[v], dbuf.at[v], dsend.at[d], drecv.at[d], at_z(v)).wait_recv()

    for r in range(rb):
        block = dbuf[r * per:(r + 1) * per, :, 0:D].reshape(TB, D).astype(F32)
        dnt[r] = block.T.astype(LOW)

    def backward(t, carry):
        row, col, flag = tile_scalars(t)
        dn = dbuf[pl.ds(row * per, per)].reshape(TB, D + TB)
        dnr = dnt[row]
        grads = []
        sums = []
        for half in range(2):
            lhs = jnp.concatenate([dn[:, half * TB:(half + 1) * TB], dn[:, D:D + TB]], axis=1)
            rhs = jnp.concatenate([vmask[t, half], onehot[half]], axis=1)
            dsig = mm_nt(lhs, rhs)
            for k in range(HALF):
                kk = half * HALF + k
                dl = dsig[:, k * TB:(k + 1) * TB] * gate32[t, kk]
                gate32[t, kk] = dl
                sums.append(jnp.sum(dl, axis=0, keepdims=True))
                grads.append(mm(dnr[kk * SH:(kk + 1) * SH, :], gate16[t, kk]))
        stack = jnp.concatenate(grads + sums + [jnp.zeros((TB - HEADS, TB), F32)], axis=0).astype(LOW)
        pt[t] = mm(wproj[...], stack).T
        return carry

    lax.fori_loop(0, slots, backward, 0)

    span = ny // cbx
    home = y // span
    turn = sorted(range(cbx), key=lambda o: (-min(o, cbx - o), o))

    def column(m, i):
        def one(xi, carry):
            block = xi * cbx + m
            total = pt[lut[block, 0]]
            for r in range(1, rb):
                total += pt[lut[block, r]]
            dpart[xi, pl.ds(m * span, span)] = total.astype(LOW).reshape(span, 2, nd, D)
            return carry

        lax.fori_loop(0, nx, one, 0)
        part = pl.ds(m * span, span)
        remote(
            dpart.at[:, part, 1 - c], rcore.at[:, part], bcsend.at[i], bcrecv.at[i], sibling
        ).start()

    for i, o in enumerate(turn):
        column(lax.rem(home + o, cbx), i)
    for i, o in enumerate(turn):
        m = lax.rem(home + o, cbx)
        part = pl.ds(m * span, span)
        remote(rcore.at[:, part], rcore.at[:, part], bcsend.at[i], bcrecv.at[i], sibling).wait_recv()
        s1[:, part] = (dpart[:, part, c].astype(F32) + rcore[:, part].astype(F32)).astype(LOW)
        for j in range(span):
            v = m * span + j
            for e in reversed(nearx):
                w = lax.rem(x + e, nx)
                remote(
                    s1.at[w, v], rx.at[e, v], bxsend.at[e, i * span + j], bxrecv.at[e, i * span + j], at_x(w)
                ).start()

    def edges(t, carry):
        dt = jnp.zeros((TB, TB), F32)
        for half in range(2):
            lows = []
            for k in range(HALF):
                kk = half * HALF + k
                dl = gate32[t, kk]
                egbuf[t, kk] = (dl * scale_ref[kk]).astype(LOW)
                lows.append(dl.astype(LOW))
            dt += mm(jnp.concatenate(lows, axis=1), onehot[half])
        dtbuf[t] = dt
        pltpu.make_async_copy(egbuf.at[t], edge_hbm.at[0, 0, t], esem.at[t]).start()
        return carry

    lax.fori_loop(0, slots, edges, 0)
    for r in range(rb):
        total = jnp.zeros((TB, TB), F32)
        for t in range(slots):
            total += dtbuf[t] * jnp.where(rows[t] == r, 1.0, 0.0).astype(F32)
        dtsend[r * per:(r + 1) * per] = total.astype(LOW).reshape(per, nd, TB)
    for e in farz:
        w = lax.rem(z + e, nz)
        remote(dtsend.at[w], dtrecv.at[e], gsend.at[e], grecv.at[e], at_z(w)).start()

    for i, o in enumerate(turn):
        m = lax.rem(home + o, cbx)
        for j in range(span):
            v = m * span + j
            total = s1[x, v].astype(F32)
            for e in nearx:
                remote(
                    rx.at[e, v], rx.at[e, v], bxsend.at[e, i * span + j], bxrecv.at[e, i * span + j], sibling
                ).wait_recv()
                total += rx[e, v].astype(F32)
            s2[v] = total.astype(LOW)

            @pl.when(v != y)
            def _():
                n = lax.rem(y + ny - v, ny)
                remote(s2.at[v], ry.at[n], bysend.at[n], byrecv.at[n], at_y(v)).start()

    dt = dtsend[z].astype(F32)
    for d in range(1, nz):
        remote(dtrecv.at[d], dtrecv.at[d], gsend.at[d], grecv.at[d], at_z(z)).wait_recv()
        dt += dtrecv[d].astype(F32)
    own_grad = own_grad + mm(dt.astype(LOW), wtt)
    final = s2[y].astype(F32)
    for d in range(1, ny):
        remote(ry.at[d], ry.at[d], bysend.at[d], byrecv.at[d], at_y(y)).wait_recv()
        final += ry[d].astype(F32)
    grad_ref[...] = own_grad + final

    for d in range(1, ny):
        remote(h_ref, h_ref, ysend.at[d], yrecv.at[d], sibling).wait_send()
        remote(s2.at[y], s2.at[y], bysend.at[d], byrecv.at[d], sibling).wait_send()
    for d in range(ny):
        for e in range(1, nx):
            remote(h_ref, h_ref, xsend.at[e, d], xrecv.at[e, d], sibling).wait_send()
            remote(s2.at[y], s2.at[y], bxsend.at[e, d], bxrecv.at[e, d], sibling).wait_send()
        for e in range(nx):
            remote(h_ref, h_ref, csend.at[e, d], crecv.at[e, d], sibling).wait_send()
    for i in range(cbx):
        part = pl.ds(i * span, span)
        remote(rcore.at[:, part], rcore.at[:, part], bcsend.at[i], bcrecv.at[i], sibling).wait_send()
    for d in range(1, nz):
        remote(tbuf.at[z], tbuf.at[z], tsend.at[d], trecv.at[d], sibling).wait_send()
        remote(send0.at[z], send0.at[z], z0send.at[d], z0recv.at[d], sibling).wait_send()
        remote(send1.at[z], send1.at[z], z1send.at[d], z1recv.at[d], sibling).wait_send()
        remote(dbuf.at[z], dbuf.at[z], dsend.at[d], drecv.at[d], sibling).wait_send()
        remote(dtsend.at[z], dtsend.at[z], gsend.at[d], grecv.at[d], sibling).wait_send()
    for t in range(slots):
        pltpu.make_async_copy(egbuf.at[t], edge_hbm.at[0, 0, t], esem.at[t]).wait()


def flush_kernel(out_ref, grad_ref, edge_ref, out_hbm, grad_hbm, edge_hbm, out, grad, edge, isem, osem):
    slots = edge.shape[0]
    pairs = [(edge_ref.at[0, 0, t], edge.at[t], edge_hbm.at[0, 0, t]) for t in range(slots)]
    pairs += [(out_ref, out, out_hbm), (grad_ref, grad, grad_hbm)]
    reads = [pltpu.make_async_copy(a, b, isem.at[i]) for i, (a, b, _) in enumerate(pairs)]
    writes = [pltpu.make_async_copy(b, c, osem.at[i]) for i, (_, b, c) in enumerate(pairs)]
    for copy in reads:
        copy.start()
    for read, write in zip(reads, writes):
        read.wait()
        write.start()
    for copy in writes:
        copy.wait()


def body(
    nx, ny,
    node_hidden_state, self_projection_weight, weight_value, weight_edge, weight_target,
    layer_norm_gain, edge_scale, tile_index, tile_count, edge_feature, edge_mask, cotangent,
):
    nd = node_hidden_state.shape[0]
    nz = lax.axis_size("src")
    slots = edge_mask.shape[2]
    rb = nz * nd // TB
    cb = nx * ny * 2 * nd // TB
    cbx = cb // nx
    vmem = pl.BlockSpec(memory_space=pltpu.VMEM)
    hbm = pl.BlockSpec(memory_space=pltpu.HBM)
    free = pl.BlockSpec(memory_space=pl.ANY)
    scratch = [
        pltpu.SMEM((HEADS,), F32),
        pltpu.SMEM((1, 1, 2, slots), jnp.int32),
        pltpu.SMEM((1, 1), jnp.int32),
        pltpu.VMEM((nd, D), LOW),
        pltpu.VMEM((nd, D), LOW),
        pltpu.VMEM((HEADS, D), LOW),
        pltpu.VMEM((HEADS, D), LOW),
        pltpu.VMEM((1, D), F32),
        pltpu.VMEM((D, D), LOW),
        pltpu.VMEM((D, D), LOW),
        pltpu.VMEM((slots, HEADS, TB, TB), LOW),
        pltpu.VMEM((slots, TB, TB), jnp.int32),
        pltpu.VMEM((nx, ny, 2, nd, D), LOW),
        pltpu.VMEM((nz, nd, TB), LOW),
        pltpu.VMEM((slots, HEADS, TB, TB), F32),
        pltpu.VMEM((slots, HEADS, TB, TB), LOW),
        pltpu.VMEM((slots, 2, HALF * TB, TB), LOW),
        pltpu.VMEM((2, slots, TB, D), F32),
        pltpu.VMEM((2, HALF * TB, TB), LOW),
        pltpu.VMEM((2, TB, HALF * TB), LOW),
        pltpu.VMEM((nz, nd, TB), LOW),
        pltpu.VMEM((nz, nd, D), LOW),
        pltpu.VMEM((nz, nd, TB), LOW),
        pltpu.VMEM((nz, nd, D), LOW),
        pltpu.VMEM((nz, nd, D + TB), LOW),
        pltpu.VMEM((rb, D, TB), LOW),
        pltpu.VMEM((slots, HEADS, TB, TB), LOW),
        pltpu.VMEM((slots + 1, TB, D), F32),
        pltpu.VMEM((D, D + TB), LOW),
        pltpu.SMEM((cb, rb), jnp.int32),
        pltpu.VMEM((slots, TB, TB), F32),
        pltpu.VMEM((nx, ny, 2, nd, D), LOW),
        pltpu.VMEM((nx, ny, nd, D), LOW),
        pltpu.VMEM((nx, ny, nd, D), LOW),
        pltpu.VMEM((nx, ny, nd, D), LOW),
        pltpu.VMEM((ny, nd, D), LOW),
        pltpu.VMEM((ny, nd, D), LOW),
        pltpu.VMEM((nz, nd, TB), LOW),
        pltpu.VMEM((nz, nd, TB), LOW),
        pltpu.SemaphoreType.DMA((12,)),
        pltpu.SemaphoreType.DMA((slots,)),
    ]
    for n in (
        (ny,), (nx, ny), (nx, ny), (nz,), (nz,), (nz,), (nz,), (cbx,), (nx, ny), (ny,), (nz,)
    ):
        scratch += [pltpu.SemaphoreType.DMA(n), pltpu.SemaphoreType.DMA(n)]
    shapes = (
        jax.ShapeDtypeStruct((nd, D), LOW),
        jax.ShapeDtypeStruct((nd, D), F32),
        jax.ShapeDtypeStruct((1, 1, slots, HEADS, TB, TB), LOW),
    )
    results = pl.pallas_call(
        functools.partial(kernel, (nx, ny, nz, nd, slots)),
        out_shape=shapes,
        in_specs=[hbm] * 12,
        out_specs=(vmem, vmem, free),
        scratch_shapes=scratch,
        compiler_params=pltpu.CompilerParams(
            collective_id=0, has_side_effects=True, vmem_limit_bytes=64 * 1024 * 1024
        ),
        name="gated_conv",
    )(
        edge_scale, tile_index.transpose(0, 1, 3, 2), tile_count,
        node_hidden_state, cotangent, weight_edge.T, weight_target.T, layer_norm_gain[None, :],
        self_projection_weight, weight_value, edge_feature, edge_mask,
    )
    return pl.pallas_call(
        flush_kernel,
        out_shape=shapes,
        in_specs=[free] * 3,
        out_specs=(hbm, hbm, hbm),
        scratch_shapes=[
            pltpu.VMEM((nd, D), LOW),
            pltpu.VMEM((nd, D), F32),
            pltpu.VMEM((slots, HEADS, TB, TB), LOW),
            pltpu.SemaphoreType.DMA((slots + 2,)),
            pltpu.SemaphoreType.DMA((slots + 2,)),
        ],
        compiler_params=pltpu.CompilerParams(vmem_limit_bytes=64 * 1024 * 1024),
        name="flush",
    )(*results)


def build(mesh, nx, ny):
    placed = (
        P(("dst", "src"), None), P(), P(), P(), P(), P(), P(),
        P("dst", "src", None, None), P("dst", "src"),
        P("dst", "src", None, None, None, None), P("dst", "src", None, None, None),
        P(("dst", "src"), None),
    )
    return jax.shard_map(
        functools.partial(body, nx, ny),
        mesh=mesh,
        in_specs=placed,
        out_specs=(
            P(("dst", "src"), None),
            P(("dst", "src"), None),
            P("dst", "src", None, None, None, None),
        ),
        check_vma=False,
    )


def solution(mesh):
    return build(mesh, 4, 8)
```

```python
import functools

import jax
import jax.numpy as jnp
from jax import lax
from jax.experimental import pallas as pl
from jax.experimental.pallas import tpu as pltpu
from jax.sharding import PartitionSpec as P

F32 = jnp.float32
LOW = jnp.bfloat16
D = 256
HEADS = 8
HALF = 4
UP = 4
UF = 4
UB = 4
UE = 4
TB = 128
SH = D // HEADS
MESH = pl.DeviceIdType.MESH
NT = (((1,), (1,)), ((), ()))


def mm(a, b):
    return jnp.dot(a, b, preferred_element_type=F32)


def mm_nt(a, b):
    return lax.dot_general(a, b, NT, preferred_element_type=F32)


def mm_exact(a, b):
    return jnp.dot(a, b, preferred_element_type=F32, precision=lax.Precision.HIGHEST)


def iota(shape, dim):
    return lax.broadcasted_iota(jnp.int32, shape, dim)


def kernel(
    shape,
    scale_hbm, pair_hbm, count_hbm,
    h_hbm, cot_hbm, wet_hbm, wtt_hbm, gain_hbm,
    wself_hbm, wvalue_hbm, feat_hbm, mask_hbm,
    out_ref, grad_ref, edge_hbm,
    scale_ref, pair_ref, count_ref, h_ref, cot_ref, wet_ref, wtt_ref, gain_ref,
    wself, wvalue, feat, mask, hbuf, tbuf, gate32, gate16, vmask, vals, vmaskt, srcs, nt, onehot, onehott, spread,
    send0, send1, recv0, recv1, dbuf, ddbuf, dnt, egbuf, pt, wproj, lut, dtbuf,
    dpart, rcore, s1, rx, s2, ry, dtsend, dtrecv,
    lsem, esem,
    ysend, yrecv, xsend, xrecv, csend, crecv, tsend, trecv,
    z0send, z0recv, z1send, z1recv, dsend, drecv,
    bcsend, bcrecv, bxsend, bxrecv, bysend, byrecv, gsend, grecv,
):
    nx, ny, nz, nd, slots = shape
    rb = nz * nd // TB
    cb = nx * ny * 2 * nd // TB
    cbx = cb // nx
    dst = lax.axis_index("dst")
    z = lax.axis_index("src")
    x = dst // (ny * 2)
    y = lax.rem(dst // 2, ny)
    c = lax.rem(dst, 2)

    def at_y(v):
        return {"dst": (x * ny + v) * 2 + c, "src": z}

    def at_x(v):
        return {"dst": (v * ny + y) * 2 + c, "src": z}

    def at_z(v):
        return {"dst": dst, "src": v}

    sibling = {"dst": (x * ny + y) * 2 + 1 - c, "src": z}

    def remote(src, dst_ref, ssem, rsem, device):
        return pltpu.make_async_remote_copy(
            src_ref=src, dst_ref=dst_ref, send_sem=ssem, recv_sem=rsem,
            device_id=device, device_id_type=MESH,
        )

    small = [
        pltpu.make_async_copy(a, b, lsem.at[4 + i])
        for i, (a, b) in enumerate((
            (h_hbm, h_ref), (wtt_hbm, wtt_ref), (wet_hbm, wet_ref), (pair_hbm, pair_ref),
            (count_hbm, count_ref), (scale_hbm, scale_ref), (cot_hbm, cot_ref), (gain_hbm, gain_ref),
        ))
    ]
    for load in small:
        load.start()
    loads = [
        pltpu.make_async_copy(wvalue_hbm, wvalue, lsem.at[0]),
        pltpu.make_async_copy(wself_hbm, wself, lsem.at[1]),
        pltpu.make_async_copy(mask_hbm.at[0, 0], mask, lsem.at[2]),
        pltpu.make_async_copy(feat_hbm.at[0, 0], feat, lsem.at[3]),
    ]
    for load in loads:
        load.start()

    barrier = pltpu.get_barrier_semaphore()
    for d in range(1, ny):
        pl.semaphore_signal(barrier, inc=1, device_id=at_y(lax.rem(y + d, ny)), device_id_type=MESH)
    for d in range(1, nx):
        pl.semaphore_signal(barrier, inc=1, device_id=at_x(lax.rem(x + d, nx)), device_id_type=MESH)
    for d in range(1, nz):
        pl.semaphore_signal(barrier, inc=1, device_id=at_z(lax.rem(z + d, nz)), device_id_type=MESH)
    pl.semaphore_signal(barrier, inc=1, device_id=sibling, device_id_type=MESH)

    for load in small:
        load.wait()
    h = h_ref[...]
    hbuf[x, y, c] = h
    wtt = jnp.concatenate([wtt_ref[...].astype(F32), jnp.zeros((TB - HEADS, D), F32)], axis=0).astype(LOW)
    wet32 = jnp.concatenate([wet_ref[...].astype(F32), jnp.zeros((TB - HEADS, D), F32)], axis=0)
    wet = wet32[:16].astype(LOW)
    tbuf[z] = mm_nt(h, wtt).astype(LOW)

    pl.semaphore_wait(barrier, ny + nx + nz - 2)

    near = sorted(range(1, ny), key=lambda d: (min(d, ny - d), d))
    nearx = sorted(range(1, nx), key=lambda d: (min(d, nx - d), d))
    farz = sorted(range(1, nz), key=lambda d: (-min(d, nz - d), d))
    for d in near:
        remote(h_ref, hbuf.at[x, y, c], ysend.at[d], yrecv.at[d], at_y(lax.rem(y + d, ny))).start()
    for d in farz:
        remote(tbuf.at[z], tbuf.at[z], tsend.at[d], trecv.at[d], at_z(lax.rem(z + d, nz))).start()

    def block_out(d):
        v = lax.rem(y + ny - d, ny)
        block = hbuf.at[x, v, c]
        if d:
            remote(block, block, ysend.at[d], yrecv.at[d], at_y(v)).wait_recv()
        for e in reversed(nearx):
            remote(block, block, xsend.at[e, d], xrecv.at[e, d], at_x(lax.rem(x + e, nx))).start()

    block_out(0)

    for d in near:
        block_out(d)

    count = count_ref[0, 0]
    rows = [jnp.clip(pair_ref[0, 0, 0, t], 0, rb - 1) for t in range(slots)]
    cols = [jnp.clip(pair_ref[0, 0, 1, t], 0, cb - 1) for t in range(slots)]
    live = [jnp.where(count > t, 1.0, 0.0).astype(F32) for t in range(slots)]

    def fill_lut(q, carry):
        for r in range(rb):
            found = jnp.int32(slots)
            for t in range(slots):
                hit = (rows[t] == r) & (cols[t] == q) & (count > t)
                found = jnp.where(hit, jnp.int32(t), found)
            lut[q, r] = found
        return carry

    lax.fori_loop(0, cb, fill_lut, 0)
    lane = iota((TB, TB), 1)
    for half in range(2):
        for k in range(HALF):
            onehot[half, k * TB:(k + 1) * TB, :] = jnp.where(lane == half * HALF + k, 1.0, 0.0).astype(LOW)
            here = iota((TB, TB), 0) == half * HALF + k
            spread[half, :, k * TB:(k + 1) * TB] = jnp.where(here, 0.5, 0.0).astype(LOW)
            onehott[half, :, k * TB:(k + 1) * TB] = jnp.where(here, 1.0, 0.0).astype(LOW)
    pt[slots] = jnp.zeros((TB, D), F32)
    loads[0].wait()
    wproj[0:D] = wvalue[...].astype(F32).T.astype(LOW)
    wproj[D:D + TB] = wet32.astype(LOW)
    loads[1].wait()
    self_pre = mm(h, wself[...])

    for d in [0] + near:
        v = lax.rem(y + ny - d, ny)
        for e in nearx:
            block = hbuf.at[lax.rem(x + nx - e, nx), v, c]
            remote(block, block, xsend.at[e, d], xrecv.at[e, d], sibling).wait_recv()
        row = hbuf.at[:, v, c]
        remote(row, row, csend.at[d], crecv.at[d], sibling).start()
    for d in range(1, nz):
        v = lax.rem(z + nz - d, nz)
        remote(tbuf.at[v], tbuf.at[v], tsend.at[d], trecv.at[d], at_z(v)).wait_recv()
    loads[2].wait()
    loads[3].wait()
    for d in [0] + near:
        row = hbuf.at[:, lax.rem(y + ny - d, ny), 1 - c]
        remote(row, row, csend.at[d], crecv.at[d], sibling).wait_recv()

    def h_tile(col):
        per = cbx
        xi = col // per
        q = lax.rem(col, per)
        step = ny // per
        return hbuf[xi, pl.ds(q * step, step)].reshape(TB, D)

    def tile_scalars(t):
        row = jnp.clip(pair_ref[0, 0, 0, t], 0, rb - 1)
        col = jnp.clip(pair_ref[0, 0, 1, t], 0, cb - 1)
        return row, col, jnp.where(count > t, 1.0, 0.0).astype(F32)

    lane_d = iota((TB, D), 1) // SH

    def t_rows(row):
        per = TB // nd
        return tbuf[pl.ds(row * per, per)].reshape(TB, TB)

    def prepare(t, carry):
        row, col, flag = tile_scalars(t)
        ht = h_tile(col)
        val = mm(ht, wvalue[...])
        vals[t] = val
        srcs[t] = mm_nt(wet, ht)[:HEADS].astype(LOW).astype(F32) * 0.5
        for half in range(2):
            for k in range(HALF):
                vmask[t, half, k * TB:(k + 1) * TB, :] = jnp.where(
                    lane // SH == k, val[:, half * TB:(half + 1) * TB], 0.0
                ).astype(LOW)
        return carry

    lax.fori_loop(0, slots, prepare, 0, unroll=UP)

    def forward(half):
        def step(t, carry):
            row, col, flag = tile_scalars(t)
            src = srcs[t]
            outer = mm(t_rows(row), spread[half])
            weight = mask[t].astype(F32) * flag
            gates = []
            for k in range(HALF):
                kk = half * HALF + k
                arg = feat[t, kk].astype(F32) * (scale_ref[kk] * 0.5) + (
                    outer[:, k * TB:(k + 1) * TB] + src[kk:kk + 1, :]
                )
                gate = (0.5 * jnp.tanh(arg) + 0.5) * weight
                gate32[t, kk] = gate
                low = gate.astype(LOW)
                gate16[t, kk] = low
                gates.append(low)
            rhs = jnp.concatenate([vmask[t, half], onehot[half]], axis=1)
            nt[half, t] = mm(jnp.concatenate(gates, axis=1), rhs)
            return carry

        lax.fori_loop(0, slots, step, 0, unroll=UF)

    per = TB // nd

    def row_sums(lanes, parts):
        for r in range(rb):
            sel = [jnp.where(rows[t] == r, 1.0, 0.0).astype(F32) for t in range(slots)]
            total = jnp.zeros((TB, lanes), F32)
            for half, start in parts:
                for t in range(slots):
                    total += nt[half, t, :, start:start + lanes] * sel[t]
            yield r, total

    forward(0)
    for r, total in row_sums(TB, [(0, 0)]):
        send0[r * per:(r + 1) * per] = total.astype(LOW).reshape(per, nd, TB)
    for d in farz:
        v = lax.rem(z + d, nz)
        remote(send0.at[v], recv0.at[d], z0send.at[d], z0recv.at[d], at_z(v)).start()
    forward(1)
    for r, total in row_sums(TB, [(1, 0)]):
        send1[r * per:(r + 1) * per, 0:nd] = total.astype(LOW).reshape(per, nd, TB)
    for r, total in row_sums(TB, [(0, TB), (1, TB)]):
        total = total.reshape(per, 2, nd // 2, TB)
        moved = pltpu.roll(total[:, 1].reshape(TB // 2, TB), HEADS, axis=1)
        packed = total[:, 0].reshape(TB // 2, TB) + moved
        send1[r * per:(r + 1) * per, nd:] = packed.astype(LOW).reshape(per, nd // 2, TB)
    for d in farz:
        v = lax.rem(z + d, nz)
        remote(send1.at[v], recv1.at[d], z1send.at[d], z1recv.at[d], at_z(v)).start()

    def slope(t, carry):
        for k in range(HEADS):
            g = gate32[t, k]
            gate32[t, k] = g - g * g
        for half in range(2):
            turned = vals[t, :, half * TB:(half + 1) * TB].T
            for k in range(HALF):
                vmaskt[t, half, :, k * TB:(k + 1) * TB] = jnp.where(
                    iota((TB, TB), 0) // SH == k, turned, 0.0
                ).astype(LOW)
        return carry

    lax.fori_loop(0, slots, slope, 0)

    num0 = send0[z].astype(F32)
    both = send1[z].astype(F32)
    for d in range(1, nz):
        remote(recv0.at[d], recv0.at[d], z0send.at[d], z0recv.at[d], at_z(z)).wait_recv()
        num0 += recv0[d].astype(F32)
    for d in range(1, nz):
        remote(recv1.at[d], recv1.at[d], z1send.at[d], z1recv.at[d], at_z(z)).wait_recv()
        both += recv1[d].astype(F32)

    num = jnp.concatenate([num0, both[0:nd]], axis=1)
    floor = jnp.concatenate([both[nd:], pltpu.roll(both[nd:], TB - HEADS, axis=1)], axis=0) + 1.0
    expand = jnp.where(iota((TB, D), 0) == lane_d, 1.0, 0.0).astype(F32)
    floor_d = mm_exact(floor, expand)
    pre = self_pre + num / floor_d
    centred = pre - jnp.mean(pre, axis=-1, keepdims=True)
    inv = lax.rsqrt(jnp.mean(centred * centred, axis=-1, keepdims=True) + 1e-05)
    xhat = centred * inv
    gain = gain_ref[...]
    yv = xhat * gain
    sg = jax.nn.sigmoid(yv)
    cot = cot_ref[...].astype(F32)
    out_ref[...] = (h.astype(F32) + yv * sg).astype(LOW)
    dx = cot * sg * (1.0 + yv * (1.0 - sg)) * gain
    dpre = inv * (
        dx - jnp.mean(dx, axis=-1, keepdims=True) - xhat * jnp.mean(dx * xhat, axis=-1, keepdims=True)
    )
    collect = jnp.where(iota((D, TB), 0) // SH == iota((D, TB), 1), 1.0, 0.0).astype(F32)
    dden = -mm_exact(dpre * num, collect) / (floor * floor)
    dnum = dpre / floor_d
    dbuf[z] = jnp.concatenate(
        [dnum[:, :TB], dnum[:, TB:], dden[:nd // 2] + pltpu.roll(dden[nd // 2:], HEADS, axis=1)], axis=0
    ).astype(LOW)
    for d in farz:
        remote(dbuf.at[z], dbuf.at[z], dsend.at[d], drecv.at[d], at_z(lax.rem(z + d, nz))).start()
    own_grad = cot + mm_nt(dpre.astype(LOW), wself[...])
    for d in range(1, nz):
        v = lax.rem(z + nz - d, nz)
        remote(dbuf.at[v], dbuf.at[v], dsend.at[d], drecv.at[d], at_z(v)).wait_recv()

    for r in range(rb):
        for half in range(2):
            block = dbuf[r * per:(r + 1) * per, half * nd:(half + 1) * nd].reshape(TB, TB)
            dnt[r, half * TB:(half + 1) * TB] = block.astype(F32).T.astype(LOW)
    packed = dbuf[:, 2 * nd:].astype(F32).reshape(nz * nd // 2, TB)
    ddbuf[:, :nd // 2] = packed.astype(LOW).reshape(nz, nd // 2, TB)
    ddbuf[:, nd // 2:] = pltpu.roll(packed, TB - HEADS, axis=1).astype(LOW).reshape(nz, nd // 2, TB)

    def backward(t, carry):
        row, col, flag = tile_scalars(t)
        dd = ddbuf[pl.ds(row * per, per)].reshape(TB, TB)
        dnr = dnt[row]
        grads = []
        sums = []
        for half in range(2):
            dn = dbuf[pl.ds(row * per, per), half * nd:(half + 1) * nd].reshape(TB, TB)
            lhs = jnp.concatenate([dn, dd], axis=1)
            rhs = jnp.concatenate([vmaskt[t, half], onehott[half]], axis=0)
            dsig = mm(lhs, rhs)
            for k in range(HALF):
                kk = half * HALF + k
                dl = dsig[:, k * TB:(k + 1) * TB] * gate32[t, kk]
                gate32[t, kk] = dl
                sums.append(jnp.sum(dl, axis=0, keepdims=True))
                grads.append(mm(dnr[kk * SH:(kk + 1) * SH, :], gate16[t, kk]))
        stack = jnp.concatenate(grads + sums + [jnp.zeros((TB - HEADS, TB), F32)], axis=0)
        pt[t] = mm(stack.T.astype(LOW), wproj[...])
        return carry

    lax.fori_loop(0, slots, backward, 0, unroll=UB)

    span = ny // cbx
    home = y // span
    turn = sorted(range(cbx), key=lambda o: (-min(o, cbx - o), o))

    def column(m, i):
        def one(xi, carry):
            block = xi * cbx + m
            total = pt[lut[block, 0]]
            for r in range(1, rb):
                total += pt[lut[block, r]]
            dpart[xi, pl.ds(m * span, span)] = total.astype(LOW).reshape(span, 2, nd, D)
            return carry

        lax.fori_loop(0, nx, one, 0)
        part = pl.ds(m * span, span)
        remote(
            dpart.at[:, part, 1 - c], rcore.at[:, part], bcsend.at[i], bcrecv.at[i], sibling
        ).start()

    for i, o in enumerate(turn):
        column(lax.rem(home + o, cbx), i)
    for i, o in enumerate(turn):
        m = lax.rem(home + o, cbx)
        part = pl.ds(m * span, span)
        remote(rcore.at[:, part], rcore.at[:, part], bcsend.at[i], bcrecv.at[i], sibling).wait_recv()
        s1[:, part] = (dpart[:, part, c].astype(F32) + rcore[:, part].astype(F32)).astype(LOW)
        for j in range(span):
            v = m * span + j
            for e in reversed(nearx):
                w = lax.rem(x + e, nx)
                remote(
                    s1.at[w, v], rx.at[e, v], bxsend.at[e, i * span + j], bxrecv.at[e, i * span + j], at_x(w)
                ).start()

    def edges(t, carry):
        dt = jnp.zeros((TB, TB), F32)
        for half in range(2):
            lows = []
            for k in range(HALF):
                kk = half * HALF + k
                dl = gate32[t, kk]
                egbuf[t, kk] = (dl * scale_ref[kk]).astype(LOW)
                lows.append(dl.astype(LOW))
            dt += mm(jnp.concatenate(lows, axis=1), onehot[half])
        dtbuf[t] = dt
        pltpu.make_async_copy(egbuf.at[t], edge_hbm.at[0, 0, t], esem.at[t]).start()
        return carry

    lax.fori_loop(0, slots, edges, 0, unroll=UE)
    for r in range(rb):
        total = jnp.zeros((TB, TB), F32)
        for t in range(slots):
            total += dtbuf[t] * jnp.where(rows[t] == r, 1.0, 0.0).astype(F32)
        dtsend[r * per:(r + 1) * per] = total.astype(LOW).reshape(per, nd, TB)
    for e in farz:
        w = lax.rem(z + e, nz)
        remote(dtsend.at[w], dtrecv.at[e], gsend.at[e], grecv.at[e], at_z(w)).start()

    for i, o in enumerate(turn):
        m = lax.rem(home + o, cbx)
        for j in range(span):
            v = m * span + j
            total = s1[x, v].astype(F32)
            for e in nearx:
                remote(
                    rx.at[e, v], rx.at[e, v], bxsend.at[e, i * span + j], bxrecv.at[e, i * span + j], sibling
                ).wait_recv()
                total += rx[e, v].astype(F32)
            s2[v] = total.astype(LOW)

            @pl.when(v != y)
            def _():
                n = lax.rem(y + ny - v, ny)
                remote(s2.at[v], ry.at[n], bysend.at[n], byrecv.at[n], at_y(v)).start()

    dt = dtsend[z].astype(F32)
    for d in range(1, nz):
        remote(dtrecv.at[d], dtrecv.at[d], gsend.at[d], grecv.at[d], at_z(z)).wait_recv()
        dt += dtrecv[d].astype(F32)
    own_grad = own_grad + mm(dt.astype(LOW), wtt)
    final = s2[y].astype(F32)
    for d in range(1, ny):
        remote(ry.at[d], ry.at[d], bysend.at[d], byrecv.at[d], at_y(y)).wait_recv()
        final += ry[d].astype(F32)
    grad_ref[...] = own_grad + final

    for d in range(1, ny):
        remote(h_ref, h_ref, ysend.at[d], yrecv.at[d], sibling).wait_send()
        remote(s2.at[y], s2.at[y], bysend.at[d], byrecv.at[d], sibling).wait_send()
    for d in range(ny):
        for e in range(1, nx):
            remote(h_ref, h_ref, xsend.at[e, d], xrecv.at[e, d], sibling).wait_send()
            remote(s2.at[y], s2.at[y], bxsend.at[e, d], bxrecv.at[e, d], sibling).wait_send()
        row = hbuf.at[:, y, c]
        remote(row, row, csend.at[d], crecv.at[d], sibling).wait_send()
    for i in range(cbx):
        part = pl.ds(i * span, span)
        remote(rcore.at[:, part], rcore.at[:, part], bcsend.at[i], bcrecv.at[i], sibling).wait_send()
    for d in range(1, nz):
        remote(tbuf.at[z], tbuf.at[z], tsend.at[d], trecv.at[d], sibling).wait_send()
        remote(send0.at[z], send0.at[z], z0send.at[d], z0recv.at[d], sibling).wait_send()
        remote(send1.at[z], send1.at[z], z1send.at[d], z1recv.at[d], sibling).wait_send()
        remote(dbuf.at[z], dbuf.at[z], dsend.at[d], drecv.at[d], sibling).wait_send()
        remote(dtsend.at[z], dtsend.at[z], gsend.at[d], grecv.at[d], sibling).wait_send()
    for t in range(slots):
        pltpu.make_async_copy(egbuf.at[t], edge_hbm.at[0, 0, t], esem.at[t]).wait()


def flush_kernel(out_ref, grad_ref, edge_ref, out_hbm, grad_hbm, edge_hbm, out, grad, edge, isem, osem):
    slots = edge.shape[0]
    pairs = [(edge_ref.at[0, 0, t], edge.at[t], edge_hbm.at[0, 0, t]) for t in range(slots)]
    pairs += [(out_ref, out, out_hbm), (grad_ref, grad, grad_hbm)]
    reads = [pltpu.make_async_copy(a, b, isem.at[i]) for i, (a, b, _) in enumerate(pairs)]
    writes = [pltpu.make_async_copy(b, c, osem.at[i]) for i, (_, b, c) in enumerate(pairs)]
    for copy in reads:
        copy.start()
    for read, write in zip(reads, writes):
        read.wait()
        write.start()
    for copy in writes:
        copy.wait()


def body(
    nx, ny,
    node_hidden_state, self_projection_weight, weight_value, weight_edge, weight_target,
    layer_norm_gain, edge_scale, tile_index, tile_count, edge_feature, edge_mask, cotangent,
):
    nd = node_hidden_state.shape[0]
    nz = lax.axis_size("src")
    slots = edge_mask.shape[2]
    rb = nz * nd // TB
    cb = nx * ny * 2 * nd // TB
    cbx = cb // nx
    vmem = pl.BlockSpec(memory_space=pltpu.VMEM)
    hbm = pl.BlockSpec(memory_space=pltpu.HBM)
    free = pl.BlockSpec(memory_space=pl.ANY)
    scratch = [
        pltpu.SMEM((HEADS,), F32),
        pltpu.SMEM((1, 1, 2, slots), jnp.int32),
        pltpu.SMEM((1, 1), jnp.int32),
        pltpu.VMEM((nd, D), LOW),
        pltpu.VMEM((nd, D), LOW),
        pltpu.VMEM((HEADS, D), LOW),
        pltpu.VMEM((HEADS, D), LOW),
        pltpu.VMEM((1, D), F32),
        pltpu.VMEM((D, D), LOW),
        pltpu.VMEM((D, D), LOW),
        pltpu.VMEM((slots, HEADS, TB, TB), LOW),
        pltpu.VMEM((slots, TB, TB), jnp.int32),
        pltpu.VMEM((nx, ny, 2, nd, D), LOW),
        pltpu.VMEM((nz, nd, TB), LOW),
        pltpu.VMEM((slots, HEADS, TB, TB), F32),
        pltpu.VMEM((slots, HEADS, TB, TB), LOW),
        pltpu.VMEM((slots, 2, HALF * TB, TB), LOW),
        pltpu.VMEM((slots, TB, D), F32),
        pltpu.VMEM((slots, 2, TB, HALF * TB), LOW),
        pltpu.VMEM((slots, HEADS, TB), F32),
        pltpu.VMEM((2, slots, TB, D), F32),
        pltpu.VMEM((2, HALF * TB, TB), LOW),
        pltpu.VMEM((2, TB, HALF * TB), LOW),
        pltpu.VMEM((2, TB, HALF * TB), LOW),
        pltpu.VMEM((nz, nd, TB), LOW),
        pltpu.VMEM((nz, nd + nd // 2, TB), LOW),
        pltpu.VMEM((nz, nd, TB), LOW),
        pltpu.VMEM((nz, nd + nd // 2, TB), LOW),
        pltpu.VMEM((nz, 2 * nd + nd // 2, TB), LOW),
        pltpu.VMEM((nz, nd, TB), LOW),
        pltpu.VMEM((rb, D, TB), LOW),
        pltpu.VMEM((slots, HEADS, TB, TB), LOW),
        pltpu.VMEM((slots + 1, TB, D), F32),
        pltpu.VMEM((D + TB, D), LOW),
        pltpu.SMEM((cb, rb), jnp.int32),
        pltpu.VMEM((slots, TB, TB), F32),
        pltpu.VMEM((nx, ny, 2, nd, D), LOW),
        pltpu.VMEM((nx, ny, nd, D), LOW),
        pltpu.VMEM((nx, ny, nd, D), LOW),
        pltpu.VMEM((nx, ny, nd, D), LOW),
        pltpu.VMEM((ny, nd, D), LOW),
        pltpu.VMEM((ny, nd, D), LOW),
        pltpu.VMEM((nz, nd, TB), LOW),
        pltpu.VMEM((nz, nd, TB), LOW),
        pltpu.SemaphoreType.DMA((12,)),
        pltpu.SemaphoreType.DMA((slots,)),
    ]
    for n in (
        (ny,), (nx, ny), (ny,), (nz,), (nz,), (nz,), (nz,), (cbx,), (nx, ny), (ny,), (nz,)
    ):
        scratch += [pltpu.SemaphoreType.DMA(n), pltpu.SemaphoreType.DMA(n)]
    shapes = (
        jax.ShapeDtypeStruct((nd, D), LOW),
        jax.ShapeDtypeStruct((nd, D), F32),
        jax.ShapeDtypeStruct((1, 1, slots, HEADS, TB, TB), LOW),
    )
    results = pl.pallas_call(
        functools.partial(kernel, (nx, ny, nz, nd, slots)),
        out_shape=shapes,
        in_specs=[hbm] * 12,
        out_specs=(vmem, vmem, free),
        scratch_shapes=scratch,
        compiler_params=pltpu.CompilerParams(
            collective_id=0, has_side_effects=True, vmem_limit_bytes=64 * 1024 * 1024
        ),
        name="gated_conv",
    )(
        edge_scale, tile_index.transpose(0, 1, 3, 2), tile_count,
        node_hidden_state, cotangent, weight_edge.T, weight_target.T, layer_norm_gain[None, :],
        self_projection_weight, weight_value, edge_feature, edge_mask,
    )
    return pl.pallas_call(
        flush_kernel,
        out_shape=shapes,
        in_specs=[free] * 3,
        out_specs=(hbm, hbm, hbm),
        scratch_shapes=[
            pltpu.VMEM((nd, D), LOW),
            pltpu.VMEM((nd, D), F32),
            pltpu.VMEM((slots, HEADS, TB, TB), LOW),
            pltpu.SemaphoreType.DMA((slots + 2,)),
            pltpu.SemaphoreType.DMA((slots + 2,)),
        ],
        compiler_params=pltpu.CompilerParams(vmem_limit_bytes=64 * 1024 * 1024),
        name="flush",
    )(*results)


def build(mesh, nx, ny):
    placed = (
        P(("dst", "src"), None), P(), P(), P(), P(), P(), P(),
        P("dst", "src", None, None), P("dst", "src"),
        P("dst", "src", None, None, None, None), P("dst", "src", None, None, None),
        P(("dst", "src"), None),
    )
    return jax.shard_map(
        functools.partial(body, nx, ny),
        mesh=mesh,
        in_specs=placed,
        out_specs=(
            P(("dst", "src"), None),
            P(("dst", "src"), None),
            P("dst", "src", None, None, None, None),
        ),
        check_vma=False,
    )


def solution(mesh):
    return build(mesh, 4, 8)
```

```python
import functools

import jax
import jax.numpy as jnp
from jax import lax
from jax.experimental import pallas as pl
from jax.experimental.pallas import tpu as pltpu
from jax.sharding import PartitionSpec as P

F32 = jnp.float32
LOW = jnp.bfloat16
D = 256
HEADS = 8
HALF = 4
UP = 8
UF = 4
UB = 8
UE = 4
TB = 128
SH = D // HEADS
MESH = pl.DeviceIdType.MESH
NT = (((1,), (1,)), ((), ()))


def mm(a, b):
    return jnp.dot(a, b, preferred_element_type=F32)


def mm_nt(a, b):
    return lax.dot_general(a, b, NT, preferred_element_type=F32)


def mm_exact(a, b):
    return jnp.dot(a, b, preferred_element_type=F32, precision=lax.Precision.HIGHEST)


def iota(shape, dim):
    return lax.broadcasted_iota(jnp.int32, shape, dim)


def kernel(
    shape,
    scale_hbm, pair_hbm, count_hbm,
    h_hbm, cot_hbm, wet_hbm, wtt_hbm, gain_hbm,
    wself_hbm, wvalue_hbm, feat_hbm, mask_hbm,
    out_ref, grad_ref, edge_hbm,
    scale_ref, pair_ref, count_ref, h_ref, cot_ref, wet_ref, wtt_ref, gain_ref,
    wself, wvalue, feat, mask, hbuf, tbuf, gate32, gatet, vmask, vals, vmaskt, srcs, nt, onehot, onehott, spread,
    send0, send1, recv0, recv1, dbuf, dbuf1, ddbuf, dnmask, sums, stack, egbuf, pt, wproj, lut, dtbuf,
    dpart, rcore, s1, rx, s2, ry, dtsend, dtrecv,
    lsem, esem,
    ysend, yrecv, xsend, xrecv, csend, crecv, tsend, trecv,
    z0send, z0recv, z1send, z1recv, dsend, drecv, d1send, d1recv,
    bcsend, bcrecv, bxsend, bxrecv, bysend, byrecv, gsend, grecv,
):
    nx, ny, nz, nd, slots = shape
    rb = nz * nd // TB
    cb = nx * ny * 2 * nd // TB
    cbx = cb // nx
    dst = lax.axis_index("dst")
    z = lax.axis_index("src")
    x = dst // (ny * 2)
    y = lax.rem(dst // 2, ny)
    c = lax.rem(dst, 2)

    def at_y(v):
        return {"dst": (x * ny + v) * 2 + c, "src": z}

    def at_x(v):
        return {"dst": (v * ny + y) * 2 + c, "src": z}

    def at_z(v):
        return {"dst": dst, "src": v}

    sibling = {"dst": (x * ny + y) * 2 + 1 - c, "src": z}

    def remote(src, dst_ref, ssem, rsem, device):
        return pltpu.make_async_remote_copy(
            src_ref=src, dst_ref=dst_ref, send_sem=ssem, recv_sem=rsem,
            device_id=device, device_id_type=MESH,
        )

    small = [
        pltpu.make_async_copy(a, b, lsem.at[4 + i])
        for i, (a, b) in enumerate((
            (h_hbm, h_ref), (wtt_hbm, wtt_ref), (wet_hbm, wet_ref), (pair_hbm, pair_ref),
            (count_hbm, count_ref), (scale_hbm, scale_ref), (cot_hbm, cot_ref), (gain_hbm, gain_ref),
        ))
    ]
    for load in small:
        load.start()
    loads = [
        pltpu.make_async_copy(wvalue_hbm, wvalue, lsem.at[0]),
        pltpu.make_async_copy(wself_hbm, wself, lsem.at[1]),
        pltpu.make_async_copy(mask_hbm.at[0, 0], mask, lsem.at[2]),
        pltpu.make_async_copy(feat_hbm.at[0, 0], feat, lsem.at[3]),
    ]
    for load in loads:
        load.start()

    barrier = pltpu.get_barrier_semaphore()
    for d in range(1, ny):
        pl.semaphore_signal(barrier, inc=1, device_id=at_y(lax.rem(y + d, ny)), device_id_type=MESH)
    for d in range(1, nx):
        pl.semaphore_signal(barrier, inc=1, device_id=at_x(lax.rem(x + d, nx)), device_id_type=MESH)
    for d in range(1, nz):
        pl.semaphore_signal(barrier, inc=1, device_id=at_z(lax.rem(z + d, nz)), device_id_type=MESH)
    pl.semaphore_signal(barrier, inc=1, device_id=sibling, device_id_type=MESH)

    for load in small:
        load.wait()
    h = h_ref[...]
    hbuf[x, y, c] = h
    wtt = jnp.concatenate([wtt_ref[...].astype(F32), jnp.zeros((TB - HEADS, D), F32)], axis=0).astype(LOW)
    wet32 = jnp.concatenate([wet_ref[...].astype(F32), jnp.zeros((TB - HEADS, D), F32)], axis=0)
    wet = wet32[:16].astype(LOW)
    tbuf[z] = mm_nt(h, wtt).astype(LOW)

    pl.semaphore_wait(barrier, ny + nx + nz - 2)

    near = sorted(range(1, ny), key=lambda d: (min(d, ny - d), d))
    nearx = sorted(range(1, nx), key=lambda d: (min(d, nx - d), d))
    farz = sorted(range(1, nz), key=lambda d: (-min(d, nz - d), d))
    for d in near:
        remote(h_ref, hbuf.at[x, y, c], ysend.at[d], yrecv.at[d], at_y(lax.rem(y + d, ny))).start()
    for d in farz:
        remote(tbuf.at[z], tbuf.at[z], tsend.at[d], trecv.at[d], at_z(lax.rem(z + d, nz))).start()

    def block_out(d):
        v = lax.rem(y + ny - d, ny)
        block = hbuf.at[x, v, c]
        if d:
            remote(block, block, ysend.at[d], yrecv.at[d], at_y(v)).wait_recv()
        for e in reversed(nearx):
            remote(block, block, xsend.at[e, d], xrecv.at[e, d], at_x(lax.rem(x + e, nx))).start()

    block_out(0)

    for d in near:
        block_out(d)

    count = count_ref[0, 0]
    rows = [jnp.clip(pair_ref[0, 0, 0, t], 0, rb - 1) for t in range(slots)]
    cols = [jnp.clip(pair_ref[0, 0, 1, t], 0, cb - 1) for t in range(slots)]
    live = [jnp.where(count > t, 1.0, 0.0).astype(F32) for t in range(slots)]

    def fill_lut(q, carry):
        for r in range(rb):
            found = jnp.int32(slots)
            for t in range(slots):
                hit = (rows[t] == r) & (cols[t] == q) & (count > t)
                found = jnp.where(hit, jnp.int32(t), found)
            lut[q, r] = found
        return carry

    lax.fori_loop(0, cb, fill_lut, 0)
    lane = iota((TB, TB), 1)
    for half in range(2):
        for k in range(HALF):
            onehot[half, k * TB:(k + 1) * TB, :] = jnp.where(lane == half * HALF + k, 1.0, 0.0).astype(LOW)
            here = iota((TB, TB), 0) == half * HALF + k
            spread[half, :, k * TB:(k + 1) * TB] = jnp.where(here, 0.5, 0.0).astype(LOW)
            onehott[half, :, k * TB:(k + 1) * TB] = jnp.where(here, 1.0, 0.0).astype(LOW)
    pt[slots] = jnp.zeros((TB, D), F32)
    loads[0].wait()
    wproj[0:D] = wvalue[...].astype(F32).T.astype(LOW)
    wproj[D:D + TB] = wet32.astype(LOW)
    loads[1].wait()
    self_pre = mm(h, wself[...])

    for d in [0] + near:
        v = lax.rem(y + ny - d, ny)
        for e in nearx:
            block = hbuf.at[lax.rem(x + nx - e, nx), v, c]
            remote(block, block, xsend.at[e, d], xrecv.at[e, d], sibling).wait_recv()
        row = hbuf.at[:, v, c]
        remote(row, row, csend.at[d], crecv.at[d], sibling).start()
    for d in range(1, nz):
        v = lax.rem(z + nz - d, nz)
        remote(tbuf.at[v], tbuf.at[v], tsend.at[d], trecv.at[d], at_z(v)).wait_recv()
    loads[2].wait()
    loads[3].wait()
    for d in [0] + near:
        row = hbuf.at[:, lax.rem(y + ny - d, ny), 1 - c]
        remote(row, row, csend.at[d], crecv.at[d], sibling).wait_recv()

    def h_tile(col):
        per = cbx
        xi = col // per
        q = lax.rem(col, per)
        step = ny // per
        return hbuf[xi, pl.ds(q * step, step)].reshape(TB, D)

    def tile_scalars(t):
        row = jnp.clip(pair_ref[0, 0, 0, t], 0, rb - 1)
        col = jnp.clip(pair_ref[0, 0, 1, t], 0, cb - 1)
        return row, col, jnp.where(count > t, 1.0, 0.0).astype(F32)

    lane_d = iota((TB, D), 1) // SH

    def t_rows(row):
        per = TB // nd
        return tbuf[pl.ds(row * per, per)].reshape(TB, TB)

    def prepare(t, carry):
        row, col, flag = tile_scalars(t)
        ht = h_tile(col)
        val = mm(ht, wvalue[...])
        vals[t] = val
        srcs[t] = mm_nt(wet, ht)[:HEADS].astype(LOW).astype(F32) * 0.5
        for half in range(2):
            for k in range(HALF):
                vmask[t, half, k * TB:(k + 1) * TB, :] = jnp.where(
                    lane // SH == k, val[:, half * TB:(half + 1) * TB], 0.0
                ).astype(LOW)
        return carry

    lax.fori_loop(0, slots, prepare, 0, unroll=UP)

    def forward(half):
        def step(t, carry):
            row, col, flag = tile_scalars(t)
            src = srcs[t]
            outer = mm(t_rows(row), spread[half])
            weight = mask[t].astype(F32) * flag
            gates = []
            for k in range(HALF):
                kk = half * HALF + k
                arg = feat[t, kk].astype(F32) * (scale_ref[kk] * 0.5) + (
                    outer[:, k * TB:(k + 1) * TB] + src[kk:kk + 1, :]
                )
                gate = (0.5 * jnp.tanh(arg) + 0.5) * weight
                gate32[t, kk] = gate
                gates.append(gate.astype(LOW))
            rhs = jnp.concatenate([vmask[t, half], onehot[half]], axis=1)
            nt[half, t] = mm(jnp.concatenate(gates, axis=1), rhs)
            return carry

        lax.fori_loop(0, slots, step, 0, unroll=UF)

    per = TB // nd

    def row_sums(lanes, parts):
        for r in range(rb):
            sel = [jnp.where(rows[t] == r, 1.0, 0.0).astype(F32) for t in range(slots)]
            total = jnp.zeros((TB, lanes), F32)
            for half, start in parts:
                for t in range(slots):
                    total += nt[half, t, :, start:start + lanes] * sel[t]
            yield r, total

    forward(0)
    for r, total in row_sums(TB, [(0, 0)]):
        send0[r * per:(r + 1) * per] = total.astype(LOW).reshape(per, nd, TB)
    for d in farz:
        v = lax.rem(z + d, nz)
        remote(send0.at[v], recv0.at[d], z0send.at[d], z0recv.at[d], at_z(v)).start()
    forward(1)
    for r, total in row_sums(TB, [(1, 0)]):
        send1[r * per:(r + 1) * per, 0:nd] = total.astype(LOW).reshape(per, nd, TB)
    for r, total in row_sums(TB, [(0, TB), (1, TB)]):
        total = total.reshape(per, 2, nd // 2, TB)
        moved = pltpu.roll(total[:, 1].reshape(TB // 2, TB), HEADS, axis=1)
        packed = total[:, 0].reshape(TB // 2, TB) + moved
        send1[r * per:(r + 1) * per, nd:] = packed.astype(LOW).reshape(per, nd // 2, TB)
    for d in farz:
        v = lax.rem(z + d, nz)
        remote(send1.at[v], recv1.at[d], z1send.at[d], z1recv.at[d], at_z(v)).start()

    def slope(t, carry):
        for half in range(2):
            turned = vals[t, :, half * TB:(half + 1) * TB].T
            for k in range(HALF):
                kk = half * HALF + k
                lanes = slice(k * TB, (k + 1) * TB)
                g = gate32[t, kk]
                gate32[t, kk] = g - g * g
                gatet[t, half, :, lanes] = g.T.astype(LOW)
                vmaskt[t, half, :, lanes] = jnp.where(
                    iota((TB, TB), 0) // SH == k, turned, 0.0
                ).astype(LOW)
        return carry

    lax.fori_loop(0, slots, slope, 0)

    num0 = send0[z].astype(F32)
    both = send1[z].astype(F32)
    for d in range(1, nz):
        remote(recv0.at[d], recv0.at[d], z0send.at[d], z0recv.at[d], at_z(z)).wait_recv()
        num0 += recv0[d].astype(F32)
    for d in range(1, nz):
        remote(recv1.at[d], recv1.at[d], z1send.at[d], z1recv.at[d], at_z(z)).wait_recv()
        both += recv1[d].astype(F32)

    num = jnp.concatenate([num0, both[0:nd]], axis=1)
    floor = jnp.concatenate([both[nd:], pltpu.roll(both[nd:], TB - HEADS, axis=1)], axis=0) + 1.0
    expand = jnp.where(iota((TB, D), 0) == lane_d, 1.0, 0.0).astype(F32)
    floor_d = mm_exact(floor, expand)
    pre = self_pre + num / floor_d
    centred = pre - jnp.mean(pre, axis=-1, keepdims=True)
    inv = lax.rsqrt(jnp.mean(centred * centred, axis=-1, keepdims=True) + 1e-05)
    xhat = centred * inv
    gain = gain_ref[...]
    yv = xhat * gain
    sg = jax.nn.sigmoid(yv)
    cot = cot_ref[...].astype(F32)
    out_ref[...] = (h.astype(F32) + yv * sg).astype(LOW)
    dx = cot * sg * (1.0 + yv * (1.0 - sg)) * gain
    dpre = inv * (
        dx - jnp.mean(dx, axis=-1, keepdims=True) - xhat * jnp.mean(dx * xhat, axis=-1, keepdims=True)
    )
    collect = jnp.where(iota((D, TB), 0) // SH == iota((D, TB), 1), 1.0, 0.0).astype(F32)
    dden = -mm_exact(dpre * num, collect) / (floor * floor)
    dnum = dpre / floor_d
    lead = nd + nd // 2
    dbuf[z] = jnp.concatenate(
        [dnum[:, :TB], dden[:nd // 2] + pltpu.roll(dden[nd // 2:], HEADS, axis=1)], axis=0
    ).astype(LOW)
    dbuf1[z] = dnum[:, TB:].astype(LOW)
    for part, ssem, rsem in ((dbuf, dsend, drecv), (dbuf1, d1send, d1recv)):
        for d in farz:
            block = part.at[z]
            remote(block, block, ssem.at[d], rsem.at[d], at_z(lax.rem(z + d, nz))).start()
    own_grad = cot + mm_nt(dpre.astype(LOW), wself[...])

    halves = (dbuf, dbuf1)

    def mask_rows(half):
        for r in range(rb):
            block = halves[half][r * per:(r + 1) * per, 0:nd].reshape(TB, TB).astype(F32)
            for k in range(HALF):
                dnmask[r, half, k * TB:(k + 1) * TB] = jnp.where(lane // SH == k, block, 0.0).astype(LOW)

    for d in range(1, nz):
        block = dbuf.at[lax.rem(z + nz - d, nz)]
        remote(block, block, dsend.at[d], drecv.at[d], sibling).wait_recv()
    packed = dbuf[:, nd:lead].astype(F32).reshape(nz * nd // 2, TB)
    ddbuf[:, :nd // 2] = packed.astype(LOW).reshape(nz, nd // 2, TB)
    ddbuf[:, nd // 2:] = pltpu.roll(packed, TB - HEADS, axis=1).astype(LOW).reshape(nz, nd // 2, TB)

    def backward(half):
        def step(t, carry):
            row, col, flag = tile_scalars(t)
            dd = ddbuf[pl.ds(row * per, per)].reshape(TB, TB)
            dn = halves[half][pl.ds(row * per, per), 0:nd].reshape(TB, TB)
            rhs = jnp.concatenate([vmaskt[t, half], onehott[half]], axis=0)
            dsig = mm(jnp.concatenate([dn, dd], axis=1), rhs)
            for k in range(HALF):
                kk = half * HALF + k
                dl = dsig[:, k * TB:(k + 1) * TB] * gate32[t, kk]
                gate32[t, kk] = dl
                sums[t, kk:kk + 1] = jnp.sum(dl, axis=0, keepdims=True)
            stack[t, :, half * TB:(half + 1) * TB] = mm(gatet[t, half], dnmask[row, half]).astype(LOW)
            if half == 1:
                dg = jnp.concatenate([sums[t], jnp.zeros((TB - HEADS, TB), F32)], axis=0)
                stack[t, :, D:] = dg.T.astype(LOW)
            return carry

        lax.fori_loop(0, slots, step, 0, unroll=UB)

    mask_rows(0)
    backward(0)
    for d in range(1, nz):
        block = dbuf1.at[lax.rem(z + nz - d, nz)]
        remote(block, block, d1send.at[d], d1recv.at[d], sibling).wait_recv()
    mask_rows(1)
    backward(1)
    pt[:slots] = mm(stack[...].reshape(slots * TB, D + TB), wproj[...]).reshape(slots, TB, D)

    span = ny // cbx
    home = y // span
    turn = sorted(range(cbx), key=lambda o: (-min(o, cbx - o), o))

    def column(m, i):
        def one(xi, carry):
            block = xi * cbx + m
            total = pt[lut[block, 0]]
            for r in range(1, rb):
                total += pt[lut[block, r]]
            dpart[xi, pl.ds(m * span, span)] = total.astype(LOW).reshape(span, 2, nd, D)
            return carry

        lax.fori_loop(0, nx, one, 0)
        part = pl.ds(m * span, span)
        remote(
            dpart.at[:, part, 1 - c], rcore.at[:, part], bcsend.at[i], bcrecv.at[i], sibling
        ).start()

    for i, o in enumerate(turn):
        column(lax.rem(home + o, cbx), i)
    for i, o in enumerate(turn):
        m = lax.rem(home + o, cbx)
        part = pl.ds(m * span, span)
        remote(rcore.at[:, part], rcore.at[:, part], bcsend.at[i], bcrecv.at[i], sibling).wait_recv()
        s1[:, part] = (dpart[:, part, c].astype(F32) + rcore[:, part].astype(F32)).astype(LOW)
        for j in range(span):
            v = m * span + j
            for e in reversed(nearx):
                w = lax.rem(x + e, nx)
                remote(
                    s1.at[w, v], rx.at[e, v], bxsend.at[e, i * span + j], bxrecv.at[e, i * span + j], at_x(w)
                ).start()

    def edges(t, carry):
        dt = jnp.zeros((TB, TB), F32)
        for half in range(2):
            lows = []
            for k in range(HALF):
                kk = half * HALF + k
                dl = gate32[t, kk]
                egbuf[t, kk] = (dl * scale_ref[kk]).astype(LOW)
                lows.append(dl.astype(LOW))
            dt += mm(jnp.concatenate(lows, axis=1), onehot[half])
        dtbuf[t] = dt
        pltpu.make_async_copy(egbuf.at[t], edge_hbm.at[0, 0, t], esem.at[t]).start()
        return carry

    lax.fori_loop(0, slots, edges, 0, unroll=UE)
    for r in range(rb):
        total = jnp.zeros((TB, TB), F32)
        for t in range(slots):
            total += dtbuf[t] * jnp.where(rows[t] == r, 1.0, 0.0).astype(F32)
        dtsend[r * per:(r + 1) * per] = total.astype(LOW).reshape(per, nd, TB)
    for e in farz:
        w = lax.rem(z + e, nz)
        remote(dtsend.at[w], dtrecv.at[e], gsend.at[e], grecv.at[e], at_z(w)).start()

    for i, o in enumerate(turn):
        m = lax.rem(home + o, cbx)
        for j in range(span):
            v = m * span + j
            total = s1[x, v].astype(F32)
            for e in nearx:
                remote(
                    rx.at[e, v], rx.at[e, v], bxsend.at[e, i * span + j], bxrecv.at[e, i * span + j], sibling
                ).wait_recv()
                total += rx[e, v].astype(F32)
            s2[v] = total.astype(LOW)

            @pl.when(v != y)
            def _():
                n = lax.rem(y + ny - v, ny)
                remote(s2.at[v], ry.at[n], bysend.at[n], byrecv.at[n], at_y(v)).start()

    dt = dtsend[z].astype(F32)
    for d in range(1, nz):
        remote(dtrecv.at[d], dtrecv.at[d], gsend.at[d], grecv.at[d], at_z(z)).wait_recv()
        dt += dtrecv[d].astype(F32)
    own_grad = own_grad + mm(dt.astype(LOW), wtt)
    final = s2[y].astype(F32)
    for d in range(1, ny):
        remote(h_ref, h_ref, ysend.at[d], yrecv.at[d], sibling).wait_send()
    for d in range(ny):
        for e in range(1, nx):
            remote(h_ref, h_ref, xsend.at[e, d], xrecv.at[e, d], sibling).wait_send()
            remote(s2.at[y], s2.at[y], bxsend.at[e, d], bxrecv.at[e, d], sibling).wait_send()
        row = hbuf.at[:, y, c]
        remote(row, row, csend.at[d], crecv.at[d], sibling).wait_send()
    for i in range(cbx):
        part = pl.ds(i * span, span)
        remote(rcore.at[:, part], rcore.at[:, part], bcsend.at[i], bcrecv.at[i], sibling).wait_send()
    for d in range(1, nz):
        remote(tbuf.at[z], tbuf.at[z], tsend.at[d], trecv.at[d], sibling).wait_send()
        remote(send0.at[z], send0.at[z], z0send.at[d], z0recv.at[d], sibling).wait_send()
        remote(send1.at[z], send1.at[z], z1send.at[d], z1recv.at[d], sibling).wait_send()
        remote(dbuf.at[z], dbuf.at[z], dsend.at[d], drecv.at[d], sibling).wait_send()
        remote(dbuf1.at[z], dbuf1.at[z], d1send.at[d], d1recv.at[d], sibling).wait_send()
        remote(dtsend.at[z], dtsend.at[z], gsend.at[d], grecv.at[d], sibling).wait_send()
    for t in range(slots):
        pltpu.make_async_copy(egbuf.at[t], edge_hbm.at[0, 0, t], esem.at[t]).wait()

    for d in range(1, ny):
        remote(ry.at[d], ry.at[d], bysend.at[d], byrecv.at[d], at_y(y)).wait_recv()
        final += ry[d].astype(F32)
    grad_ref[...] = own_grad + final

    for d in range(1, ny):
        remote(s2.at[y], s2.at[y], bysend.at[d], byrecv.at[d], sibling).wait_send()


def flush_kernel(out_ref, grad_ref, edge_ref, out_hbm, grad_hbm, edge_hbm, out, grad, edge, isem, osem):
    slots = edge.shape[0]
    pairs = [(edge_ref.at[0, 0, t], edge.at[t], edge_hbm.at[0, 0, t]) for t in range(slots)]
    pairs += [(out_ref, out, out_hbm), (grad_ref, grad, grad_hbm)]
    reads = [pltpu.make_async_copy(a, b, isem.at[i]) for i, (a, b, _) in enumerate(pairs)]
    writes = [pltpu.make_async_copy(b, c, osem.at[i]) for i, (_, b, c) in enumerate(pairs)]
    for copy in reads:
        copy.start()
    for read, write in zip(reads, writes):
        read.wait()
        write.start()
    for copy in writes:
        copy.wait()


def body(
    nx, ny,
    node_hidden_state, self_projection_weight, weight_value, weight_edge, weight_target,
    layer_norm_gain, edge_scale, tile_index, tile_count, edge_feature, edge_mask, cotangent,
):
    nd = node_hidden_state.shape[0]
    nz = lax.axis_size("src")
    slots = edge_mask.shape[2]
    rb = nz * nd // TB
    cb = nx * ny * 2 * nd // TB
    cbx = cb // nx
    vmem = pl.BlockSpec(memory_space=pltpu.VMEM)
    hbm = pl.BlockSpec(memory_space=pltpu.HBM)
    free = pl.BlockSpec(memory_space=pl.ANY)
    scratch = [
        pltpu.SMEM((HEADS,), F32),
        pltpu.SMEM((1, 1, 2, slots), jnp.int32),
        pltpu.SMEM((1, 1), jnp.int32),
        pltpu.VMEM((nd, D), LOW),
        pltpu.VMEM((nd, D), LOW),
        pltpu.VMEM((HEADS, D), LOW),
        pltpu.VMEM((HEADS, D), LOW),
        pltpu.VMEM((1, D), F32),
        pltpu.VMEM((D, D), LOW),
        pltpu.VMEM((D, D), LOW),
        pltpu.VMEM((slots, HEADS, TB, TB), LOW),
        pltpu.VMEM((slots, TB, TB), jnp.int32),
        pltpu.VMEM((nx, ny, 2, nd, D), LOW),
        pltpu.VMEM((nz, nd, TB), LOW),
        pltpu.VMEM((slots, HEADS, TB, TB), F32),
        pltpu.VMEM((slots, 2, TB, HALF * TB), LOW),
        pltpu.VMEM((slots, 2, HALF * TB, TB), LOW),
        pltpu.VMEM((slots, TB, D), F32),
        pltpu.VMEM((slots, 2, TB, HALF * TB), LOW),
        pltpu.VMEM((slots, HEADS, TB), F32),
        pltpu.VMEM((2, slots, TB, D), F32),
        pltpu.VMEM((2, HALF * TB, TB), LOW),
        pltpu.VMEM((2, TB, HALF * TB), LOW),
        pltpu.VMEM((2, TB, HALF * TB), LOW),
        pltpu.VMEM((nz, nd, TB), LOW),
        pltpu.VMEM((nz, nd + nd // 2, TB), LOW),
        pltpu.VMEM((nz, nd, TB), LOW),
        pltpu.VMEM((nz, nd + nd // 2, TB), LOW),
        pltpu.VMEM((nz, nd + nd // 2, TB), LOW),
        pltpu.VMEM((nz, nd, TB), LOW),
        pltpu.VMEM((nz, nd, TB), LOW),
        pltpu.VMEM((rb, 2, HALF * TB, TB), LOW),
        pltpu.VMEM((slots, HEADS, TB), F32),
        pltpu.VMEM((slots, TB, D + TB), LOW),
        pltpu.VMEM((slots, HEADS, TB, TB), LOW),
        pltpu.VMEM((slots + 1, TB, D), F32),
        pltpu.VMEM((D + TB, D), LOW),
        pltpu.SMEM((cb, rb), jnp.int32),
        pltpu.VMEM((slots, TB, TB), F32),
        pltpu.VMEM((nx, ny, 2, nd, D), LOW),
        pltpu.VMEM((nx, ny, nd, D), LOW),
        pltpu.VMEM((nx, ny, nd, D), LOW),
        pltpu.VMEM((nx, ny, nd, D), LOW),
        pltpu.VMEM((ny, nd, D), LOW),
        pltpu.VMEM((ny, nd, D), LOW),
        pltpu.VMEM((nz, nd, TB), LOW),
        pltpu.VMEM((nz, nd, TB), LOW),
        pltpu.SemaphoreType.DMA((12,)),
        pltpu.SemaphoreType.DMA((slots,)),
    ]
    for n in (
        (ny,), (nx, ny), (ny,), (nz,), (nz,), (nz,), (nz,), (nz,), (cbx,), (nx, ny), (ny,), (nz,)
    ):
        scratch += [pltpu.SemaphoreType.DMA(n), pltpu.SemaphoreType.DMA(n)]
    shapes = (
        jax.ShapeDtypeStruct((nd, D), LOW),
        jax.ShapeDtypeStruct((nd, D), F32),
        jax.ShapeDtypeStruct((1, 1, slots, HEADS, TB, TB), LOW),
    )
    results = pl.pallas_call(
        functools.partial(kernel, (nx, ny, nz, nd, slots)),
        out_shape=shapes,
        in_specs=[hbm] * 12,
        out_specs=(vmem, vmem, free),
        scratch_shapes=scratch,
        compiler_params=pltpu.CompilerParams(
            collective_id=0, has_side_effects=True, vmem_limit_bytes=64 * 1024 * 1024
        ),
        name="gated_conv",
    )(
        edge_scale, tile_index.transpose(0, 1, 3, 2), tile_count,
        node_hidden_state, cotangent, weight_edge.T, weight_target.T, layer_norm_gain[None, :],
        self_projection_weight, weight_value, edge_feature, edge_mask,
    )
    return pl.pallas_call(
        flush_kernel,
        out_shape=shapes,
        in_specs=[free] * 3,
        out_specs=(hbm, hbm, hbm),
        scratch_shapes=[
            pltpu.VMEM((nd, D), LOW),
            pltpu.VMEM((nd, D), F32),
            pltpu.VMEM((slots, HEADS, TB, TB), LOW),
            pltpu.SemaphoreType.DMA((slots + 2,)),
            pltpu.SemaphoreType.DMA((slots + 2,)),
        ],
        compiler_params=pltpu.CompilerParams(vmem_limit_bytes=64 * 1024 * 1024),
        name="flush",
    )(*results)


def build(mesh, nx, ny):
    placed = (
        P(("dst", "src"), None), P(), P(), P(), P(), P(), P(),
        P("dst", "src", None, None), P("dst", "src"),
        P("dst", "src", None, None, None, None), P("dst", "src", None, None, None),
        P(("dst", "src"), None),
    )
    return jax.shard_map(
        functools.partial(body, nx, ny),
        mesh=mesh,
        in_specs=placed,
        out_specs=(
            P(("dst", "src"), None),
            P(("dst", "src"), None),
            P("dst", "src", None, None, None, None),
        ),
        check_vma=False,
    )


def solution(mesh):
    return build(mesh, 4, 8)
```

```python
import functools

import jax
import jax.numpy as jnp
from jax import lax
from jax.experimental import pallas as pl
from jax.experimental.pallas import tpu as pltpu
from jax.sharding import PartitionSpec as P

F32 = jnp.float32
LOW = jnp.bfloat16
D = 256
HEADS = 8
HALF = 4
UP = 8
UF = 4
UB = 8
UE = 4
TB = 128
SH = D // HEADS
MESH = pl.DeviceIdType.MESH
NT = (((1,), (1,)), ((), ()))


def mm(a, b):
    return jnp.dot(a, b, preferred_element_type=F32)


def mm_nt(a, b):
    return lax.dot_general(a, b, NT, preferred_element_type=F32)


def mm_exact(a, b):
    return jnp.dot(a, b, preferred_element_type=F32, precision=lax.Precision.HIGHEST)


def iota(shape, dim):
    return lax.broadcasted_iota(jnp.int32, shape, dim)


def kernel(
    shape,
    scale_hbm, pair_hbm, count_hbm,
    h_hbm, cot_hbm, wet_hbm, wtt_hbm, gain_hbm,
    wself_hbm, wvalue_hbm, feat_hbm, mask_hbm,
    out_ref, grad_ref, edge_hbm,
    scale_ref, pair_ref, count_ref, h_ref, cot_ref, wet_ref, wtt_ref, gain_ref,
    wself, wvalue, feat, mask, hbuf, tbuf, gate32, gatet, vmask, vals, vmaskt, srcs, nt, onehot, onehott, spread,
    send0, send1, recv0, recv1, dbuf, dbuf1, ddbuf, dnmask, sums, stack, egbuf, pt, wproj, lut, dtbuf,
    dpart, rcore, s1, rx, s2, ry, dtsend, dtrecv,
    lsem, esem,
    ysend, yrecv, xsend, xrecv, csend, crecv, tsend, trecv,
    z0send, z0recv, z1send, z1recv, dsend, drecv, d1send, d1recv,
    bcsend, bcrecv, bxsend, bxrecv, bysend, byrecv, gsend, grecv,
):
    nx, ny, nz, nd, slots = shape
    rb = nz * nd // TB
    cb = nx * ny * 2 * nd // TB
    cbx = cb // nx
    dst = lax.axis_index("dst")
    z = lax.axis_index("src")
    x = dst // (ny * 2)
    y = lax.rem(dst // 2, ny)
    c = lax.rem(dst, 2)

    def at_y(v):
        return {"dst": (x * ny + v) * 2 + c, "src": z}

    def at_x(v):
        return {"dst": (v * ny + y) * 2 + c, "src": z}

    def at_z(v):
        return {"dst": dst, "src": v}

    sibling = {"dst": (x * ny + y) * 2 + 1 - c, "src": z}

    def remote(src, dst_ref, ssem, rsem, device):
        return pltpu.make_async_remote_copy(
            src_ref=src, dst_ref=dst_ref, send_sem=ssem, recv_sem=rsem,
            device_id=device, device_id_type=MESH,
        )

    small = [
        pltpu.make_async_copy(a, b, lsem.at[4 + i])
        for i, (a, b) in enumerate((
            (h_hbm, h_ref), (wtt_hbm, wtt_ref), (wet_hbm, wet_ref), (pair_hbm, pair_ref),
            (count_hbm, count_ref), (scale_hbm, scale_ref), (cot_hbm, cot_ref), (gain_hbm, gain_ref),
        ))
    ]
    for load in small:
        load.start()
    loads = [
        pltpu.make_async_copy(wvalue_hbm, wvalue, lsem.at[0]),
        pltpu.make_async_copy(wself_hbm, wself, lsem.at[1]),
        pltpu.make_async_copy(mask_hbm.at[0, 0], mask, lsem.at[2]),
        pltpu.make_async_copy(feat_hbm.at[0, 0], feat, lsem.at[3]),
    ]
    for load in loads:
        load.start()

    barrier = pltpu.get_barrier_semaphore()
    for d in range(1, ny):
        pl.semaphore_signal(barrier, inc=1, device_id=at_y(lax.rem(y + d, ny)), device_id_type=MESH)
    for d in range(1, nx):
        pl.semaphore_signal(barrier, inc=1, device_id=at_x(lax.rem(x + d, nx)), device_id_type=MESH)
    for d in range(1, nz):
        pl.semaphore_signal(barrier, inc=1, device_id=at_z(lax.rem(z + d, nz)), device_id_type=MESH)
    pl.semaphore_signal(barrier, inc=1, device_id=sibling, device_id_type=MESH)

    for load in small:
        load.wait()
    h = h_ref[...]
    hbuf[x, y, c] = h
    wtt = jnp.concatenate([wtt_ref[...].astype(F32), jnp.zeros((TB - HEADS, D), F32)], axis=0).astype(LOW)
    wet32 = jnp.concatenate([wet_ref[...].astype(F32), jnp.zeros((TB - HEADS, D), F32)], axis=0)
    wet = wet32[:16].astype(LOW)
    tbuf[z] = mm_nt(h, wtt).astype(LOW)

    pl.semaphore_wait(barrier, ny + nx + nz - 2)

    near = sorted(range(1, ny), key=lambda d: (min(d, ny - d), d))
    nearx = sorted(range(1, nx), key=lambda d: (min(d, nx - d), d))
    farz = sorted(range(1, nz), key=lambda d: (-min(d, nz - d), d))
    for d in near:
        remote(h_ref, hbuf.at[x, y, c], ysend.at[d], yrecv.at[d], at_y(lax.rem(y + d, ny))).start()
    for d in farz:
        remote(tbuf.at[z], tbuf.at[z], tsend.at[d], trecv.at[d], at_z(lax.rem(z + d, nz))).start()

    def block_out(d):
        v = lax.rem(y + ny - d, ny)
        block = hbuf.at[x, v, c]
        if d:
            remote(block, block, ysend.at[d], yrecv.at[d], at_y(v)).wait_recv()
        for e in reversed(nearx):
            remote(block, block, xsend.at[e, d], xrecv.at[e, d], at_x(lax.rem(x + e, nx))).start()

    block_out(0)

    for d in near:
        block_out(d)

    count = count_ref[0, 0]
    rows = [jnp.clip(pair_ref[0, 0, 0, t], 0, rb - 1) for t in range(slots)]
    cols = [jnp.clip(pair_ref[0, 0, 1, t], 0, cb - 1) for t in range(slots)]
    live = [jnp.where(count > t, 1.0, 0.0).astype(F32) for t in range(slots)]

    def fill_lut(q, carry):
        for r in range(rb):
            found = jnp.int32(slots)
            for t in range(slots):
                hit = (rows[t] == r) & (cols[t] == q) & (count > t)
                found = jnp.where(hit, jnp.int32(t), found)
            lut[q, r] = found
        return carry

    lax.fori_loop(0, cb, fill_lut, 0)
    lane = iota((TB, TB), 1)
    for half in range(2):
        for k in range(HALF):
            onehot[half, k * TB:(k + 1) * TB, :] = jnp.where(lane == half * HALF + k, 1.0, 0.0).astype(LOW)
            here = iota((TB, TB), 0) == half * HALF + k
            spread[half, :, k * TB:(k + 1) * TB] = jnp.where(here, 0.5, 0.0).astype(LOW)
            onehott[half, :, k * TB:(k + 1) * TB] = jnp.where(here, 1.0, 0.0).astype(LOW)
    pt[slots] = jnp.zeros((TB, D), F32)
    loads[0].wait()
    wproj[0:D] = wvalue[...].astype(F32).T.astype(LOW)
    wproj[D:D + TB] = wet32.astype(LOW)
    loads[1].wait()
    self_pre = mm(h, wself[...])

    for d in [0] + near:
        v = lax.rem(y + ny - d, ny)
        for e in nearx:
            block = hbuf.at[lax.rem(x + nx - e, nx), v, c]
            remote(block, block, xsend.at[e, d], xrecv.at[e, d], sibling).wait_recv()
        row = hbuf.at[:, v, c]
        remote(row, row, csend.at[d], crecv.at[d], sibling).start()
    for d in range(1, nz):
        v = lax.rem(z + nz - d, nz)
        remote(tbuf.at[v], tbuf.at[v], tsend.at[d], trecv.at[d], at_z(v)).wait_recv()
    loads[2].wait()
    loads[3].wait()
    for d in [0] + near:
        row = hbuf.at[:, lax.rem(y + ny - d, ny), 1 - c]
        remote(row, row, csend.at[d], crecv.at[d], sibling).wait_recv()

    def h_tile(col):
        per = cbx
        xi = col // per
        q = lax.rem(col, per)
        step = ny // per
        return hbuf[xi, pl.ds(q * step, step)].reshape(TB, D)

    def tile_scalars(t):
        row = jnp.clip(pair_ref[0, 0, 0, t], 0, rb - 1)
        col = jnp.clip(pair_ref[0, 0, 1, t], 0, cb - 1)
        return row, col, jnp.where(count > t, 1.0, 0.0).astype(F32)

    lane_d = iota((TB, D), 1) // SH

    def t_rows(row):
        per = TB // nd
        return tbuf[pl.ds(row * per, per)].reshape(TB, TB)

    def prepare(t, carry):
        row, col, flag = tile_scalars(t)
        ht = h_tile(col)
        val = mm(ht, wvalue[...])
        vals[t] = val
        srcs[t] = mm_nt(wet, ht)[:HEADS].astype(LOW).astype(F32) * 0.5
        for half in range(2):
            for k in range(HALF):
                vmask[t, half, k * TB:(k + 1) * TB, :] = jnp.where(
                    lane // SH == k, val[:, half * TB:(half + 1) * TB], 0.0
                ).astype(LOW)
        return carry

    lax.fori_loop(0, slots, prepare, 0, unroll=UP)

    def forward(half):
        def step(t, carry):
            row, col, flag = tile_scalars(t)
            src = srcs[t]
            outer = mm(t_rows(row), spread[half])
            weight = mask[t].astype(F32) * flag
            gates = []
            for k in range(HALF):
                kk = half * HALF + k
                arg = feat[t, kk].astype(F32) * (scale_ref[kk] * 0.5) + (
                    outer[:, k * TB:(k + 1) * TB] + src[kk:kk + 1, :]
                )
                gate = (0.5 * jnp.tanh(arg) + 0.5) * weight
                gate32[t, kk] = gate
                gates.append(gate.astype(LOW))
            rhs = jnp.concatenate([vmask[t, half], onehot[half]], axis=1)
            nt[half, t] = mm(jnp.concatenate(gates, axis=1), rhs)
            return carry

        lax.fori_loop(0, slots, step, 0, unroll=UF)

    per = TB // nd

    def row_sums(lanes, parts):
        for r in range(rb):
            sel = [jnp.where(rows[t] == r, 1.0, 0.0).astype(F32) for t in range(slots)]
            total = jnp.zeros((TB, lanes), F32)
            for half, start in parts:
                for t in range(slots):
                    total += nt[half, t, :, start:start + lanes] * sel[t]
            yield r, total

    forward(0)
    for r, total in row_sums(TB, [(0, 0)]):
        send0[r * per:(r + 1) * per] = total.astype(LOW).reshape(per, nd, TB)
    for d in farz:
        v = lax.rem(z + d, nz)
        remote(send0.at[v], recv0.at[d], z0send.at[d], z0recv.at[d], at_z(v)).start()
    forward(1)
    for r, total in row_sums(TB, [(1, 0)]):
        send1[r * per:(r + 1) * per, 0:nd] = total.astype(LOW).reshape(per, nd, TB)
    for r, total in row_sums(TB, [(0, TB), (1, TB)]):
        total = total.reshape(per, 2, nd // 2, TB)
        moved = pltpu.roll(total[:, 1].reshape(TB // 2, TB), HEADS, axis=1)
        packed = total[:, 0].reshape(TB // 2, TB) + moved
        send1[r * per:(r + 1) * per, nd:] = packed.astype(LOW).reshape(per, nd // 2, TB)
    for d in farz:
        v = lax.rem(z + d, nz)
        remote(send1.at[v], recv1.at[d], z1send.at[d], z1recv.at[d], at_z(v)).start()

    def slope(t, carry):
        for half in range(2):
            turned = vals[t, :, half * TB:(half + 1) * TB].T
            for k in range(HALF):
                kk = half * HALF + k
                lanes = slice(k * TB, (k + 1) * TB)
                g = gate32[t, kk]
                gate32[t, kk] = g - g * g
                gatet[t, half, :, lanes] = g.T.astype(LOW)
                vmaskt[t, half, :, lanes] = jnp.where(
                    iota((TB, TB), 0) // SH == k, turned, 0.0
                ).astype(LOW)
        return carry

    lax.fori_loop(0, slots, slope, 0)

    num0 = send0[z].astype(F32)
    both = send1[z].astype(F32)
    for d in range(1, nz):
        remote(recv0.at[d], recv0.at[d], z0send.at[d], z0recv.at[d], at_z(z)).wait_recv()
        num0 += recv0[d].astype(F32)
    for d in range(1, nz):
        remote(recv1.at[d], recv1.at[d], z1send.at[d], z1recv.at[d], at_z(z)).wait_recv()
        both += recv1[d].astype(F32)

    num = jnp.concatenate([num0, both[0:nd]], axis=1)
    floor = jnp.concatenate([both[nd:], pltpu.roll(both[nd:], TB - HEADS, axis=1)], axis=0) + 1.0
    expand = jnp.where(iota((TB, D), 0) == lane_d, 1.0, 0.0).astype(F32)
    floor_d = mm_exact(floor, expand)
    pre = self_pre + num / floor_d
    centred = pre - jnp.mean(pre, axis=-1, keepdims=True)
    inv = lax.rsqrt(jnp.mean(centred * centred, axis=-1, keepdims=True) + 1e-05)
    xhat = centred * inv
    gain = gain_ref[...]
    yv = xhat * gain
    sg = jax.nn.sigmoid(yv)
    cot = cot_ref[...].astype(F32)
    out_ref[...] = (h.astype(F32) + yv * sg).astype(LOW)
    dx = cot * sg * (1.0 + yv * (1.0 - sg)) * gain
    dpre = inv * (
        dx - jnp.mean(dx, axis=-1, keepdims=True) - xhat * jnp.mean(dx * xhat, axis=-1, keepdims=True)
    )
    collect = jnp.where(iota((D, TB), 0) // SH == iota((D, TB), 1), 1.0, 0.0).astype(F32)
    dden = -mm_exact(dpre * num, collect) / (floor * floor)
    dnum = dpre / floor_d
    lead = nd + nd // 2
    dbuf[z] = jnp.concatenate(
        [dnum[:, :TB], dden[:nd // 2] + pltpu.roll(dden[nd // 2:], HEADS, axis=1)], axis=0
    ).astype(LOW)
    dbuf1[z] = dnum[:, TB:].astype(LOW)
    for part, ssem, rsem in ((dbuf, dsend, drecv), (dbuf1, d1send, d1recv)):
        for d in farz:
            block = part.at[z]
            remote(block, block, ssem.at[d], rsem.at[d], at_z(lax.rem(z + d, nz))).start()
    own_grad = cot + mm_nt(dpre.astype(LOW), wself[...])

    halves = (dbuf, dbuf1)

    def mask_rows(half):
        for r in range(rb):
            block = halves[half][r * per:(r + 1) * per, 0:nd].reshape(TB, TB).astype(F32)
            for k in range(HALF):
                dnmask[r, half, k * TB:(k + 1) * TB] = jnp.where(lane // SH == k, block, 0.0).astype(LOW)

    for d in range(1, nz):
        block = dbuf.at[lax.rem(z + nz - d, nz)]
        remote(block, block, dsend.at[d], drecv.at[d], sibling).wait_recv()
    packed = dbuf[:, nd:lead].astype(F32).reshape(nz * nd // 2, TB)
    ddbuf[:, :nd // 2] = packed.astype(LOW).reshape(nz, nd // 2, TB)
    ddbuf[:, nd // 2:] = pltpu.roll(packed, TB - HEADS, axis=1).astype(LOW).reshape(nz, nd // 2, TB)

    def backward(half):
        def step(t, carry):
            row, col, flag = tile_scalars(t)
            dd = ddbuf[pl.ds(row * per, per)].reshape(TB, TB)
            dn = halves[half][pl.ds(row * per, per), 0:nd].reshape(TB, TB)
            rhs = jnp.concatenate([vmaskt[t, half], onehott[half]], axis=0)
            dsig = mm(jnp.concatenate([dn, dd], axis=1), rhs)
            for k in range(HALF):
                kk = half * HALF + k
                dl = dsig[:, k * TB:(k + 1) * TB] * gate32[t, kk]
                gate32[t, kk] = dl
                sums[t, kk:kk + 1] = jnp.sum(dl, axis=0, keepdims=True)
            stack[t, :, half * TB:(half + 1) * TB] = mm(gatet[t, half], dnmask[row, half]).astype(LOW)
            if half == 1:
                dg = jnp.concatenate([sums[t], jnp.zeros((TB - HEADS, TB), F32)], axis=0)
                stack[t, :, D:] = dg.T.astype(LOW)
            return carry

        lax.fori_loop(0, slots, step, 0, unroll=UB)

    mask_rows(0)
    backward(0)
    for d in range(1, nz):
        block = dbuf1.at[lax.rem(z + nz - d, nz)]
        remote(block, block, d1send.at[d], d1recv.at[d], sibling).wait_recv()
    mask_rows(1)
    backward(1)
    pt[:slots] = mm(stack[...].reshape(slots * TB, D + TB), wproj[...]).reshape(slots, TB, D)

    span = ny // cbx
    home = y // span
    turn = sorted(range(cbx), key=lambda o: (-min(o, cbx - o), o))

    def column(m, i):
        def one(xi, carry):
            block = xi * cbx + m
            total = pt[lut[block, 0]]
            for r in range(1, rb):
                total += pt[lut[block, r]]
            dpart[xi, pl.ds(m * span, span)] = total.astype(LOW).reshape(span, 2, nd, D)
            return carry

        lax.fori_loop(0, nx, one, 0)
        part = pl.ds(m * span, span)
        remote(
            dpart.at[:, part, 1 - c], rcore.at[:, part], bcsend.at[i], bcrecv.at[i], sibling
        ).start()

    for i, o in enumerate(turn):
        column(lax.rem(home + o, cbx), i)
    for i, o in enumerate(turn):
        m = lax.rem(home + o, cbx)
        part = pl.ds(m * span, span)
        remote(rcore.at[:, part], rcore.at[:, part], bcsend.at[i], bcrecv.at[i], sibling).wait_recv()
        s1[:, part] = (dpart[:, part, c].astype(F32) + rcore[:, part].astype(F32)).astype(LOW)
        for j in range(span):
            v = m * span + j
            for e in reversed(nearx):
                w = lax.rem(x + e, nx)
                remote(
                    s1.at[w, v], rx.at[e, v], bxsend.at[e, i * span + j], bxrecv.at[e, i * span + j], at_x(w)
                ).start()

    def targets(t, carry):
        dt = jnp.zeros((TB, TB), F32)
        for half in range(2):
            lows = [gate32[t, half * HALF + k].astype(LOW) for k in range(HALF)]
            dt += mm(jnp.concatenate(lows, axis=1), onehot[half])
        dtbuf[t] = dt
        return carry

    lax.fori_loop(0, slots, targets, 0, unroll=UE)
    for r in range(rb):
        total = jnp.zeros((TB, TB), F32)
        for t in range(slots):
            total += dtbuf[t] * jnp.where(rows[t] == r, 1.0, 0.0).astype(F32)
        dtsend[r * per:(r + 1) * per] = total.astype(LOW).reshape(per, nd, TB)
    for e in farz:
        w = lax.rem(z + e, nz)
        remote(dtsend.at[w], dtrecv.at[e], gsend.at[e], grecv.at[e], at_z(w)).start()

    def edges(t, carry):
        for k in range(HEADS):
            egbuf[t, k] = (gate32[t, k] * scale_ref[k]).astype(LOW)
        pltpu.make_async_copy(egbuf.at[t], edge_hbm.at[0, 0, t], esem.at[t]).start()
        return carry

    lax.fori_loop(0, slots, edges, 0, unroll=UE)

    for i, o in enumerate(turn):
        m = lax.rem(home + o, cbx)
        for j in range(span):
            v = m * span + j
            total = s1[x, v].astype(F32)
            for e in nearx:
                remote(
                    rx.at[e, v], rx.at[e, v], bxsend.at[e, i * span + j], bxrecv.at[e, i * span + j], sibling
                ).wait_recv()
                total += rx[e, v].astype(F32)
            s2[v] = total.astype(LOW)

            @pl.when(v != y)
            def _():
                n = lax.rem(y + ny - v, ny)
                remote(s2.at[v], ry.at[n], bysend.at[n], byrecv.at[n], at_y(v)).start()

    dt = dtsend[z].astype(F32)
    for d in range(1, nz):
        remote(dtrecv.at[d], dtrecv.at[d], gsend.at[d], grecv.at[d], at_z(z)).wait_recv()
        dt += dtrecv[d].astype(F32)
    own_grad = own_grad + mm(dt.astype(LOW), wtt)
    final = s2[y].astype(F32)
    for d in range(1, ny):
        remote(h_ref, h_ref, ysend.at[d], yrecv.at[d], sibling).wait_send()
    for d in range(ny):
        for e in range(1, nx):
            remote(h_ref, h_ref, xsend.at[e, d], xrecv.at[e, d], sibling).wait_send()
            remote(s2.at[y], s2.at[y], bxsend.at[e, d], bxrecv.at[e, d], sibling).wait_send()
        row = hbuf.at[:, y, c]
        remote(row, row, csend.at[d], crecv.at[d], sibling).wait_send()
    for i in range(cbx):
        part = pl.ds(i * span, span)
        remote(rcore.at[:, part], rcore.at[:, part], bcsend.at[i], bcrecv.at[i], sibling).wait_send()
    for d in range(1, nz):
        remote(tbuf.at[z], tbuf.at[z], tsend.at[d], trecv.at[d], sibling).wait_send()
        remote(send0.at[z], send0.at[z], z0send.at[d], z0recv.at[d], sibling).wait_send()
        remote(send1.at[z], send1.at[z], z1send.at[d], z1recv.at[d], sibling).wait_send()
        remote(dbuf.at[z], dbuf.at[z], dsend.at[d], drecv.at[d], sibling).wait_send()
        remote(dbuf1.at[z], dbuf1.at[z], d1send.at[d], d1recv.at[d], sibling).wait_send()
        remote(dtsend.at[z], dtsend.at[z], gsend.at[d], grecv.at[d], sibling).wait_send()
    for t in range(slots):
        pltpu.make_async_copy(egbuf.at[t], edge_hbm.at[0, 0, t], esem.at[t]).wait()

    for d in range(1, ny):
        remote(ry.at[d], ry.at[d], bysend.at[d], byrecv.at[d], at_y(y)).wait_recv()
        final += ry[d].astype(F32)
    grad_ref[...] = own_grad + final

    for d in range(1, ny):
        remote(s2.at[y], s2.at[y], bysend.at[d], byrecv.at[d], sibling).wait_send()


def flush_kernel(out_ref, grad_ref, edge_ref, out_hbm, grad_hbm, edge_hbm, out, grad, edge, isem, osem):
    slots = edge.shape[0]
    pairs = [
        (edge_ref.at[0, 0, t], edge.at[t], edge_hbm.at[0, 0, t])
        for t in (pl.ds(i, 1) for i in range(0, slots, 1))
    ]
    pairs += [(out_ref, out, out_hbm), (grad_ref, grad, grad_hbm)]
    reads = [pltpu.make_async_copy(a, b, isem.at[i]) for i, (a, b, _) in enumerate(pairs)]
    writes = [pltpu.make_async_copy(b, c, osem.at[i]) for i, (_, b, c) in enumerate(pairs)]
    for copy in reads:
        copy.start()
    for read, write in zip(reads, writes):
        read.wait()
        write.start()
    for copy in writes:
        copy.wait()


def body(
    nx, ny,
    node_hidden_state, self_projection_weight, weight_value, weight_edge, weight_target,
    layer_norm_gain, edge_scale, tile_index, tile_count, edge_feature, edge_mask, cotangent,
):
    nd = node_hidden_state.shape[0]
    nz = lax.axis_size("src")
    slots = edge_mask.shape[2]
    rb = nz * nd // TB
    cb = nx * ny * 2 * nd // TB
    cbx = cb // nx
    vmem = pl.BlockSpec(memory_space=pltpu.VMEM)
    hbm = pl.BlockSpec(memory_space=pltpu.HBM)
    free = pl.BlockSpec(memory_space=pl.ANY)
    scratch = [
        pltpu.SMEM((HEADS,), F32),
        pltpu.SMEM((1, 1, 2, slots), jnp.int32),
        pltpu.SMEM((1, 1), jnp.int32),
        pltpu.VMEM((nd, D), LOW),
        pltpu.VMEM((nd, D), LOW),
        pltpu.VMEM((HEADS, D), LOW),
        pltpu.VMEM((HEADS, D), LOW),
        pltpu.VMEM((1, D), F32),
        pltpu.VMEM((D, D), LOW),
        pltpu.VMEM((D, D), LOW),
        pltpu.VMEM((slots, HEADS, TB, TB), LOW),
        pltpu.VMEM((slots, TB, TB), jnp.int32),
        pltpu.VMEM((nx, ny, 2, nd, D), LOW),
        pltpu.VMEM((nz, nd, TB), LOW),
        pltpu.VMEM((slots, HEADS, TB, TB), F32),
        pltpu.VMEM((slots, 2, TB, HALF * TB), LOW),
        pltpu.VMEM((slots, 2, HALF * TB, TB), LOW),
        pltpu.VMEM((slots, TB, D), F32),
        pltpu.VMEM((slots, 2, TB, HALF * TB), LOW),
        pltpu.VMEM((slots, HEADS, TB), F32),
        pltpu.VMEM((2, slots, TB, D), F32),
        pltpu.VMEM((2, HALF * TB, TB), LOW),
        pltpu.VMEM((2, TB, HALF * TB), LOW),
        pltpu.VMEM((2, TB, HALF * TB), LOW),
        pltpu.VMEM((nz, nd, TB), LOW),
        pltpu.VMEM((nz, nd + nd // 2, TB), LOW),
        pltpu.VMEM((nz, nd, TB), LOW),
        pltpu.VMEM((nz, nd + nd // 2, TB), LOW),
        pltpu.VMEM((nz, nd + nd // 2, TB), LOW),
        pltpu.VMEM((nz, nd, TB), LOW),
        pltpu.VMEM((nz, nd, TB), LOW),
        pltpu.VMEM((rb, 2, HALF * TB, TB), LOW),
        pltpu.VMEM((slots, HEADS, TB), F32),
        pltpu.VMEM((slots, TB, D + TB), LOW),
        pltpu.VMEM((slots, HEADS, TB, TB), LOW),
        pltpu.VMEM((slots + 1, TB, D), F32),
        pltpu.VMEM((D + TB, D), LOW),
        pltpu.SMEM((cb, rb), jnp.int32),
        pltpu.VMEM((slots, TB, TB), F32),
        pltpu.VMEM((nx, ny, 2, nd, D), LOW),
        pltpu.VMEM((nx, ny, nd, D), LOW),
        pltpu.VMEM((nx, ny, nd, D), LOW),
        pltpu.VMEM((nx, ny, nd, D), LOW),
        pltpu.VMEM((ny, nd, D), LOW),
        pltpu.VMEM((ny, nd, D), LOW),
        pltpu.VMEM((nz, nd, TB), LOW),
        pltpu.VMEM((nz, nd, TB), LOW),
        pltpu.SemaphoreType.DMA((12,)),
        pltpu.SemaphoreType.DMA((slots,)),
    ]
    for n in (
        (ny,), (nx, ny), (ny,), (nz,), (nz,), (nz,), (nz,), (nz,), (cbx,), (nx, ny), (ny,), (nz,)
    ):
        scratch += [pltpu.SemaphoreType.DMA(n), pltpu.SemaphoreType.DMA(n)]
    shapes = (
        jax.ShapeDtypeStruct((nd, D), LOW),
        jax.ShapeDtypeStruct((nd, D), F32),
        jax.ShapeDtypeStruct((1, 1, slots, HEADS, TB, TB), LOW),
    )
    results = pl.pallas_call(
        functools.partial(kernel, (nx, ny, nz, nd, slots)),
        out_shape=shapes,
        in_specs=[hbm] * 12,
        out_specs=(vmem, vmem, free),
        scratch_shapes=scratch,
        compiler_params=pltpu.CompilerParams(
            collective_id=0, has_side_effects=True, vmem_limit_bytes=64 * 1024 * 1024
        ),
        name="gated_conv",
    )(
        edge_scale, tile_index.transpose(0, 1, 3, 2), tile_count,
        node_hidden_state, cotangent, weight_edge.T, weight_target.T, layer_norm_gain[None, :],
        self_projection_weight, weight_value, edge_feature, edge_mask,
    )
    return pl.pallas_call(
        flush_kernel,
        out_shape=shapes,
        in_specs=[free] * 3,
        out_specs=(hbm, hbm, hbm),
        scratch_shapes=[
            pltpu.VMEM((nd, D), LOW),
            pltpu.VMEM((nd, D), F32),
            pltpu.VMEM((slots, HEADS, TB, TB), LOW),
            pltpu.SemaphoreType.DMA((slots + 2,)),
            pltpu.SemaphoreType.DMA((slots + 2,)),
        ],
        compiler_params=pltpu.CompilerParams(vmem_limit_bytes=64 * 1024 * 1024),
        name="flush",
    )(*results)


def build(mesh, nx, ny):
    placed = (
        P(("dst", "src"), None), P(), P(), P(), P(), P(), P(),
        P("dst", "src", None, None), P("dst", "src"),
        P("dst", "src", None, None, None, None), P("dst", "src", None, None, None),
        P(("dst", "src"), None),
    )
    return jax.shard_map(
        functools.partial(body, nx, ny),
        mesh=mesh,
        in_specs=placed,
        out_specs=(
            P(("dst", "src"), None),
            P(("dst", "src"), None),
            P("dst", "src", None, None, None, None),
        ),
        check_vma=False,
    )


def solution(mesh):
    return build(mesh, 4, 8)
```
